512 devices in a mesh: wide: 128 (over z, y, core), tm: 4 (over x).
Axes of the slice: x: 4, y: 4, z: 16, core: 2. Of those that a mesh axis runs over, the one named last changes fastest.
Arguments:
- voltages: bfloat16 [2, 1024, 131072], P(None, 'wide', 'tm'), may hold values from -6 to 6
- filter_taps: float32 [12, 256], replicated, may hold values from -1.75 to 1.75
- stations: int32 [4, 128], replicated, may hold values from 0 to 511, as said below
- allocation: int32 [4, 256], replicated, may hold values 0 or 1
Outputs:
- visibilities: float32 [4, 256, 2, 256, 256], P('tm', 'wide')
The draws below stay inside these ranges and needn't reach their ends.
Inputs may be any that keep to these rules, and one draw needn't show every extreme that they name: `stations`: every station belongs to exactly one subarray.
All inputs are finite; a program needn't handle non-finite values.
Results may differ from the reference program's by a relative error of at most 0.0039.
Values may be sent and summed in bfloat16 or wider, within the bound.
No kernel may reach another device: no remote copies, remote signals or barrier semaphores. Data moves between devices by JAX's collectives and lax.ppermute only.
A program may use at most 64 MiB of HBM per device.

```python
import math
import jax
import jax.numpy as jnp
from jax import lax

C = 256
TAPS = 12
STA_DEV = 4
F = 128
SUBS = 4
STATIONS = 512
INPUTS = 1024
SUB_ST = 128
SUBIN = 256
NSAMP = 131072
N_TM = 4


def draw_stations(key, part):
    key = jax.random.fold_in(key, 7)
    order = jax.random.permutation(key, STATIONS)
    return order.reshape(SUBS, SUB_ST).astype(jnp.int32)


def with_ends(entries, rng, low, high):
    longest = entries.shape.index(max(entries.shape))
    spots = []
    for shift in (0, 1):
        where = [jax.random.randint(jax.random.fold_in(rng, axis), (), 0, length) for axis, length in enumerate(entries.shape)]
        where[longest] = (where[longest] + shift) % entries.shape[longest]
        spots.append(tuple(where))
    return entries.at[spots[0]].set(low).at[spots[1]].set(high)


def shard_levels(key, dims, cuts, least, high):
    level, own = 1.0, jax.random.fold_in(key, 6)
    for axis_at, shards_of in cuts:
        heights = jnp.exp(jax.random.uniform(jax.random.fold_in(own, axis_at), (shards_of,), jnp.float32, least / len(cuts), high / len(cuts)))
        level = level * jnp.repeat(heights, dims[axis_at] // shards_of).reshape([-1 if axis == axis_at else 1 for axis in range(len(dims))])
    return level


def gaussian(rng, shape, spread, bound, split=(), kind=jnp.bfloat16):
    drawn = spread * jax.random.normal(rng, shape, jnp.float32)
    if split:
        drawn = drawn * shard_levels(rng, shape, split, -0.22, 0.18)
    return jnp.clip(drawn, -bound, bound).astype(kind)


def setup_inputs(seed: int = 0) -> dict:
    keys = jax.random.split(jax.random.key(seed), 5)
    return {
        "voltages": gaussian(keys[0], (2, INPUTS, NSAMP), 1.0, 6.0, ((1, 128), (2, 4))),
        "filter_taps": gaussian(keys[1], (TAPS, C), TAPS ** -0.5, 1.75, (), jnp.float32),
        "stations": draw_stations(jax.random.fold_in(keys[4], 71), 0),
        "allocation": with_ends((jax.random.randint(keys[3], (SUBS, C), 0, 2) < 1).astype(jnp.int32), jax.random.fold_in(keys[3], 1), 0, 1),
    }


def make_tables():
    grid = jnp.arange(C, dtype=jnp.int32)[:, None] * jnp.arange(C, dtype=jnp.int32)[None, :] % C
    angle = grid.astype(jnp.float32) * (2.0 * math.pi / C)
    scale = 1.0 / math.sqrt(C)
    return ((jnp.cos(angle) * scale).astype(jnp.bfloat16), (jnp.sin(angle) * scale).astype(jnp.bfloat16))

def reference(voltages, filter_taps, stations, allocation):
    cosine_lookup, sin_table = make_tables()
    cosine_broad = cosine_lookup.astype(jnp.float32)
    sine_broad = sin_table.astype(jnp.float32)
    total_frames = N_TM * F
    block = 2 * STA_DEV
    groups = INPUTS // block

    def channelize(piece):
        signal = piece.reshape(2, block, total_frames, C)
        padded = jnp.concatenate([jnp.zeros((2, block, TAPS - 1, C), jnp.bfloat16), signal], axis=2)
        summed = jnp.zeros((2, block, total_frames, C), jnp.float32)
        for tap in range(TAPS):
            summed = summed + filter_taps[tap].astype(jnp.float32) * padded[:, :, tap:tap + total_frames, :].astype(jnp.float32)
        filter_output = summed.astype(jnp.bfloat16).astype(jnp.float32)
        real_component = jnp.einsum('md,lqd->mlq', cosine_broad, filter_output[0]) + jnp.einsum('md,lqd->mlq', sine_broad, filter_output[1])
        imaginary_component = jnp.einsum('md,lqd->mlq', cosine_broad, filter_output[1]) - jnp.einsum('md,lqd->mlq', sine_broad, filter_output[0])
        return jnp.stack([real_component, imaginary_component]).astype(jnp.bfloat16)
    grouped = voltages.reshape(2, groups, block, NSAMP).transpose(1, 0, 2, 3)
    pieces = lax.map(channelize, grouped)
    spectra = pieces.transpose(1, 2, 0, 3, 4).reshape(2, C, INPUTS, total_frames)
    rows = (2 * stations[:, :, None] + jnp.arange(2, dtype=jnp.int32)[None, None, :]).reshape(SUBS, SUBIN).astype(jnp.int32)
    scale = 1.0 / total_frames

    def correlate(chan_data):
        chosen = chan_data[:, rows].astype(jnp.float32)
        real_sel = chosen[0]
        imaginary_picked = chosen[1]
        gram_real = jnp.einsum('sif,sjf->sij', real_sel, real_sel) + jnp.einsum('sif,sjf->sij', imaginary_picked, imaginary_picked)
        gram_imag = jnp.einsum('sif,sjf->sij', imaginary_picked, real_sel) - jnp.einsum('sif,sjf->sij', real_sel, imaginary_picked)
        return jnp.stack([gram_real, gram_imag], axis=1) * scale
    grams = lax.map(correlate, spectra.transpose(1, 0, 2, 3))
    grams = grams.transpose(1, 0, 2, 3, 4)
    window_weights = allocation.astype(jnp.float32)[:, :, None, None, None]
    return grams * window_weights
```

```python
import math

import jax
import jax.numpy as jnp
import numpy as np
from jax import lax
from jax.experimental import pallas as pl
from jax.experimental.pallas import tpu as pltpu
from jax.sharding import PartitionSpec as P

LANES = 128
SUBLANES = 8
BLOCK = 16


def shifted(value, axis, steps):
    count = lax.axis_size(axis)
    initial, last = (max(0, -steps), min(count, count - steps))
    return lax.ppermute(value, axis, [(source, source + steps) for source in range(initial, last)])


def transform_table(length):
    grid = np.arange(length)[:, None] * np.arange(length)[None, :] % length
    angle = grid * (2.0 * math.pi / length)
    scale = 1.0 / math.sqrt(length)
    cosine, sine = np.cos(angle) * scale, np.sin(angle) * scale
    real = np.concatenate([cosine, sine], axis=1)
    imaginary = np.concatenate([-sine, cosine], axis=1)
    table = np.stack([real, imaginary], axis=1).reshape(2 * length, 2 * length)
    return table.astype(jnp.bfloat16)


def channelize_kernel(x_ref, halo_ref, taps_ref, table_ref, out_ref, filtered, turned):
    taps, length = taps_ref.shape
    signals = x_ref.shape[1]
    frames = x_ref.shape[2] // length
    cols = length // LANES

    def load(ref, part, frame, col):
        start = pl.multiple_of((frame * cols + col) * LANES, LANES)
        return ref[part, :, pl.ds(start, LANES)].astype(jnp.float32)

    for part in range(2):
        for col in range(cols):
            weights = [
                jnp.broadcast_to(taps_ref[tap : tap + 1, col * LANES : (col + 1) * LANES], (signals, LANES))
                for tap in range(taps)
            ]

            def filter_block(window, first, part=part, col=col, weights=weights):
                for frame in range(BLOCK):
                    total = weights[0] * window[frame]
                    for tap in range(1, taps):
                        total = total + weights[tap] * window[frame + tap]
                    filtered[part, col, pl.ds(first + frame, signals, stride=frames), :] = total

            opening = [load(halo_ref, part, frame, col) for frame in range(taps - 1)]
            opening += [load(x_ref, part, frame, col) for frame in range(BLOCK)]
            filter_block(opening, 0)

            def step(block, carry, part=part, col=col, filter_block=filter_block):
                first = block * BLOCK
                window = [
                    load(x_ref, part, first - (taps - 1) + frame, col) for frame in range(BLOCK + taps - 1)
                ]
                filter_block(window, first)
                return carry

            lax.fori_loop(1, frames // BLOCK, step, 0)

    rows = table_ref.shape[0]
    for pair in range(signals // 2):
        span = slice(pair * 2 * frames, (pair + 1) * 2 * frames)
        samples = jnp.concatenate(
            [filtered[part, col, span, :] for part in range(2) for col in range(cols)], axis=1
        ).astype(jnp.bfloat16)
        spectrum = lax.dot_general(
            table_ref[...], samples, (((1,), (1,)), ((), ())), preferred_element_type=jnp.float32
        )
        for which in range(2):
            turned[pl.ds(pair * 2 + which, rows, stride=signals), :] = spectrum[
                :, which * frames : (which + 1) * frames
            ]
    out_ref[...] = turned[...].astype(jnp.bfloat16).reshape(out_ref.shape)


def channelize(signal, halo, filter_taps, table):
    _, signals, samples = signal.shape
    length = filter_taps.shape[1]
    frames = samples // length
    rows = table.shape[0]
    return pl.pallas_call(
        channelize_kernel,
        out_shape=jax.ShapeDtypeStruct((rows, signals, frames), jnp.bfloat16),
        scratch_shapes=[
            pltpu.VMEM((2, length // LANES, signals * frames, LANES), jnp.float32),
            pltpu.VMEM((rows * signals, frames), jnp.float32),
        ],
        compiler_params=pltpu.CompilerParams(vmem_limit_bytes=24 * 1024 * 1024),
        cost_estimate=pl.CostEstimate(flops=600_000_000, bytes_accessed=3_000_000, transcendentals=0),
        name="channelize",
    )(signal, halo, filter_taps, table)


def choose_kernel(pick_ref, x_ref, out_ref):
    sources, parts, signals, frames = x_ref.shape
    columns = jnp.concatenate(
        [x_ref[:, part].reshape(sources * signals, frames) for part in range(parts)], axis=1
    )
    subs, _, members, _ = out_ref.shape
    for sub in range(subs):
        chosen = jnp.dot(
            pick_ref[sub * members : (sub + 1) * members, :], columns, preferred_element_type=jnp.float32
        ).astype(jnp.bfloat16)
        for part in range(parts):
            out_ref[sub, part] = chosen[:, part * frames : (part + 1) * frames]


def choose(pick, turned, subs):
    sources, parts, signals, frames = turned.shape
    members = sources * signals // subs
    return pl.pallas_call(
        choose_kernel,
        out_shape=jax.ShapeDtypeStruct((subs, parts, members, frames), jnp.bfloat16),
        compiler_params=pltpu.CompilerParams(vmem_limit_bytes=24 * 1024 * 1024),
        cost_estimate=pl.CostEstimate(flops=1_100_000_000, bytes_accessed=4_000_000, transcendentals=0),
        name="choose",
    )(pick, turned)


def correlate_kernel(weight_ref, x_ref, out_ref):
    segments, parts, _, _ = x_ref.shape
    for channel in range(parts // 2):
        real = [x_ref[segment, 2 * channel] for segment in range(segments)]
        imag = [x_ref[segment, 2 * channel + 1] for segment in range(segments)]
        left = jnp.concatenate(real + imag, axis=1)
        turned = jnp.concatenate(imag + [-value for value in real], axis=1)
        contract = (((1,), (1,)), ((), ()))
        weight = weight_ref[channel]
        out_ref[0, channel, 0] = weight * lax.dot_general(left, left, contract, preferred_element_type=jnp.float32)
        out_ref[0, channel, 1] = weight * lax.dot_general(turned, left, contract, preferred_element_type=jnp.float32)


def correlate(weights, gathered):
    segments, parts, members, frames = gathered.shape
    return pl.pallas_call(
        correlate_kernel,
        out_shape=jax.ShapeDtypeStruct((1, parts // 2, 2, members, members), jnp.float32),
        in_specs=[pl.BlockSpec(memory_space=pltpu.SMEM), pl.BlockSpec(memory_space=pltpu.VMEM)],
        compiler_params=pltpu.CompilerParams(vmem_limit_bytes=24 * 1024 * 1024),
        cost_estimate=pl.CostEstimate(flops=600_000_000, bytes_accessed=2_000_000, transcendentals=0),
        name="correlate",
    )(weights, gathered)


def shards(voltages, filter_taps, stations, allocation):
    num_taps, length = filter_taps.shape
    signals = voltages.shape[1]
    frames = voltages.shape[2] // length
    segments = lax.axis_size("tm")
    owners = lax.axis_size("wide")
    num_subs, sub_size = stations.shape
    halo = shifted(voltages[:, :, (frames - (num_taps - 1)) * length :], "tm", 1)
    table = jnp.asarray(transform_table(length))
    spectra = channelize(voltages, halo, filter_taps, table)
    ch_dev = length // owners
    spectra = spectra.reshape(owners, 2 * ch_dev, signals, frames)
    turned = lax.all_to_all(spectra, "wide", split_axis=0, concat_axis=0, tiled=True)
    rows = (2 * stations[:, :, None] + jnp.arange(2, dtype=jnp.int32)[None, None, :]).reshape(-1, 1)
    pick = (rows == jnp.arange(owners * signals, dtype=jnp.int32)[None, :]).astype(jnp.bfloat16)
    chosen = choose(pick, turned, num_subs)
    gathered = lax.all_to_all(chosen, "tm", split_axis=0, concat_axis=0, tiled=True)
    first_chan = lax.axis_index("wide") * ch_dev
    sub = lax.axis_index("tm")
    mine = lax.dynamic_slice(allocation, (sub, first_chan), (1, ch_dev)).reshape(ch_dev)
    weights = mine.astype(jnp.float32) * (1.0 / (frames * segments))
    return correlate(weights, gathered)


def solution(mesh):
    return jax.shard_map(
        shards,
        mesh=mesh,
        in_specs=(P(None, "wide", "tm"), P(), P(), P()),
        out_specs=P("tm", "wide", None, None, None),
        check_vma=False,
    )
```

```python
import math

import jax
import jax.numpy as jnp
import numpy as np
from jax import lax
from jax.experimental import pallas as pl
from jax.experimental.pallas import tpu as pltpu
from jax.sharding import PartitionSpec as P

LANES = 128
BLOCK = 16
WIDE_FIRST = 76
TM_FIRST = 1
IN_VMEM = pl.BlockSpec(memory_space=pltpu.VMEM)
IN_HBM = pl.BlockSpec(memory_space=pltpu.HBM)
IN_SMEM = pl.BlockSpec(memory_space=pltpu.SMEM)
PARAMS = pltpu.CompilerParams(vmem_limit_bytes=24 * 1024 * 1024)
CONTRACT_LAST = (((1,), (1,)), ((), ()))


def shifted(value, axis, steps):
    count = lax.axis_size(axis)
    initial, last = (max(0, -steps), min(count, count - steps))
    return lax.ppermute(value, axis, [(source, source + steps) for source in range(initial, last)])


def member_order(count, first):
    return [(first + step) % count for step in range(count)]


def exchange(value, axis, order):
    return lax.all_to_all(value, axis, split_axis=0, concat_axis=0, tiled=True, axis_index_groups=[order])


def transform_table(length, order):
    grid = np.arange(length)[:, None] * np.arange(length)[None, :] % length
    angle = grid * (2.0 * math.pi / length)
    scale = 1.0 / math.sqrt(length)
    cosine, sine = np.cos(angle) * scale, np.sin(angle) * scale
    real = np.concatenate([cosine, sine], axis=1)
    imaginary = np.concatenate([-sine, cosine], axis=1)
    table = np.stack([real, imaginary], axis=1).reshape(len(order), -1, 2 * length)[np.asarray(order)]
    return table.reshape(2 * length, 2 * length).astype(jnp.bfloat16)


def stage_kernel(x_ref, taps_ref, table_ref, x_out, tail_out, taps_out, table_out, sems):
    length = tail_out.shape[2]
    first = x_ref.shape[2] - length
    copies = [
        pltpu.make_async_copy(x_ref.at[:, :, first:], tail_out, sems.at[0]),
        pltpu.make_async_copy(x_ref, x_out, sems.at[1]),
        pltpu.make_async_copy(taps_ref, taps_out, sems.at[2]),
        pltpu.make_async_copy(table_ref, table_out, sems.at[3]),
    ]
    for copy in copies:
        copy.start()
    for copy in copies:
        copy.wait()


def stage(voltages, filter_taps, table):
    taps, length = filter_taps.shape
    tail = voltages.shape[:2] + ((taps - 1) * length,)
    operands = [pltpu.with_memory_space_constraint(value, pltpu.HBM) for value in (voltages, filter_taps, table)]
    return pl.pallas_call(
        stage_kernel,
        in_specs=[IN_HBM] * 3,
        out_specs=[IN_VMEM] * 4,
        out_shape=[
            pltpu.VMEM(voltages.shape, voltages.dtype),
            pltpu.VMEM(tail, voltages.dtype),
            pltpu.VMEM(filter_taps.shape, filter_taps.dtype),
            pltpu.VMEM(table.shape, table.dtype),
        ],
        scratch_shapes=[pltpu.SemaphoreType.DMA((4,))],
        compiler_params=PARAMS,
        name="stage",
    )(*operands)


def load_frame(ref, part, frame, col, cols):
    start = (frame * cols + col) * LANES
    if not isinstance(start, int):
        start = pl.multiple_of(start, LANES)
    return ref[part, :, pl.ds(start, LANES)].astype(jnp.float32)


def tap_weights(taps_ref, col, signals):
    row = [taps_ref[tap : tap + 1, col * LANES : (col + 1) * LANES] for tap in range(taps_ref.shape[0])]
    return [jnp.broadcast_to(value, (signals, LANES)) for value in row]


def filter_frame(weights, window):
    total = weights[0] * window[0]
    for weight, value in zip(weights[1:], window[1:]):
        total = total + weight * value
    return total


def filter_kernel(x_ref, taps_ref, out_ref):
    taps, length = taps_ref.shape
    signals = x_ref.shape[1]
    cols = length // LANES
    frames = x_ref.shape[2] // length
    for part in range(2):
        for col in range(cols):
            weights = tap_weights(taps_ref, col, signals)

            def step(block, window, part=part, col=col, weights=weights):
                first = block * BLOCK
                window = list(window) + [
                    load_frame(x_ref, part, first + frame, col, cols) for frame in range(BLOCK)
                ]
                for frame in range(BLOCK):
                    total = filter_frame(weights, window[frame : frame + taps])
                    out_ref[part, col, pl.ds(first + frame, signals, stride=frames), :] = total
                return tuple(window[BLOCK:])

            opening = tuple(
                load_frame(x_ref, part, BLOCK - (taps - 1) + frame, col, cols) for frame in range(taps - 1)
            )
            lax.fori_loop(1, frames // BLOCK, step, opening, unroll=frames // BLOCK - 1)


def filter_body(x, filter_taps):
    _, signals, samples = x.shape
    length = filter_taps.shape[1]
    shape = (2, length // LANES, signals * (samples // length), LANES)
    return pl.pallas_call(
        filter_kernel,
        in_specs=[IN_VMEM] * 2,
        out_specs=IN_VMEM,
        out_shape=pltpu.VMEM(shape, jnp.float32),
        compiler_params=PARAMS,
        cost_estimate=pl.CostEstimate(flops=12_000_000, bytes_accessed=6_000_000, transcendentals=0),
        name="filter_body",
    )(x, filter_taps)


def transform_kernel(body_ref, halo_ref, x_ref, taps_ref, table_ref, out_ref, opening, turned):
    taps, length = taps_ref.shape
    signals = x_ref.shape[1]
    cols = length // LANES
    frames = x_ref.shape[2] // length
    for part in range(2):
        for col in range(cols):
            weights = tap_weights(taps_ref, col, signals)
            window = [load_frame(halo_ref, part, frame, col, cols) for frame in range(taps - 1)]
            window += [load_frame(x_ref, part, frame, col, cols) for frame in range(BLOCK)]
            for frame in range(BLOCK):
                total = filter_frame(weights, window[frame : frame + taps])
                opening[part, col, pl.ds(frame, signals, stride=BLOCK), :] = total

    rows = table_ref.shape[0]
    for pair in range(0, signals, 2):
        columns = []
        for part in range(2):
            for col in range(cols):
                pieces = []
                for signal in (pair, pair + 1):
                    pieces.append(opening[part, col, signal * BLOCK : (signal + 1) * BLOCK, :])
                    pieces.append(body_ref[part, col, signal * frames + BLOCK : (signal + 1) * frames, :])
                columns.append(jnp.concatenate(pieces, axis=0))
        samples = jnp.concatenate(columns, axis=1).astype(jnp.bfloat16)
        spectrum = lax.dot_general(table_ref[...], samples, CONTRACT_LAST, preferred_element_type=jnp.float32)
        for which in range(2):
            turned[pl.ds(pair + which, rows, stride=signals), :] = spectrum[
                :, which * frames : (which + 1) * frames
            ]
    out_ref[...] = turned[...].astype(jnp.bfloat16).reshape(out_ref.shape)


def transform(body, halo, x, filter_taps, table):
    taps, length = filter_taps.shape
    signals = x.shape[1]
    frames = x.shape[2] // length
    rows = table.shape[0]
    return pl.pallas_call(
        transform_kernel,
        in_specs=[IN_VMEM] * 5,
        out_specs=IN_VMEM,
        out_shape=pltpu.VMEM((rows, signals, frames), jnp.bfloat16),
        scratch_shapes=[
            pltpu.VMEM((2, length // LANES, signals * BLOCK, LANES), jnp.float32),
            pltpu.VMEM((rows * signals, frames), jnp.float32),
        ],
        compiler_params=PARAMS,
        cost_estimate=pl.CostEstimate(flops=540_000_000, bytes_accessed=4_000_000, transcendentals=0),
        name="transform",
    )(body, halo, x, filter_taps, table)


def choose_kernel(rows_ref, signal_ref, x_ref, out_ref):
    sources, parts, signals, frames = x_ref.shape
    subs, _, members, _ = out_ref.shape
    columns = jnp.concatenate(
        [x_ref[:, part].reshape(sources * signals, frames) for part in range(parts)], axis=1
    )
    held = signal_ref[...]
    for sub in range(subs):
        wanted = rows_ref[sub * members : (sub + 1) * members, :]
        pick = jnp.where(wanted == held, 1.0, 0.0).astype(jnp.bfloat16)
        chosen = jnp.dot(pick, columns, preferred_element_type=jnp.float32).astype(jnp.bfloat16)
        for part in range(parts):
            out_ref[sub, part] = chosen[:, part * frames : (part + 1) * frames]


def choose(rows, held, turned, subs):
    _, parts, _, frames = turned.shape
    return pl.pallas_call(
        choose_kernel,
        in_specs=[IN_VMEM] * 3,
        out_specs=IN_VMEM,
        out_shape=pltpu.VMEM((subs, parts, rows.shape[0] // subs, frames), jnp.bfloat16),
        compiler_params=PARAMS,
        cost_estimate=pl.CostEstimate(flops=1_100_000_000, bytes_accessed=2_000_000, transcendentals=0),
        name="choose",
    )(rows, held, turned)


def correlate_kernel(weight_ref, x_ref, out_ref, grams, sems):
    segments = x_ref.shape[0]
    copies = []
    for channel in range(out_ref.shape[1]):
        real = [x_ref[segment, 2 * channel] for segment in range(segments)]
        imag = [x_ref[segment, 2 * channel + 1] for segment in range(segments)]
        left = jnp.concatenate(real + imag, axis=1)
        turned = jnp.concatenate(imag + [-value for value in real], axis=1)
        weight = weight_ref[channel]
        for part, rows in enumerate((left, turned)):
            grams[channel, part] = weight * lax.dot_general(
                rows, left, CONTRACT_LAST, preferred_element_type=jnp.float32
            )
            copy = pltpu.make_async_copy(
                grams.at[channel, part], out_ref.at[0, channel, part], sems.at[2 * channel + part]
            )
            copy.start()
            copies.append(copy)
    for copy in copies:
        copy.wait()


def correlate(weights, gathered):
    _, parts, members, _ = gathered.shape
    shape = (parts // 2, 2, members, members)
    return pl.pallas_call(
        correlate_kernel,
        in_specs=[IN_SMEM, IN_VMEM],
        out_specs=IN_HBM,
        out_shape=jax.ShapeDtypeStruct((1,) + shape, jnp.float32),
        scratch_shapes=[pltpu.VMEM(shape, jnp.float32), pltpu.SemaphoreType.DMA((parts,))],
        compiler_params=PARAMS,
        cost_estimate=pl.CostEstimate(flops=540_000_000, bytes_accessed=2_000_000, transcendentals=0),
        name="correlate",
    )(weights, gathered)


def shards(voltages, filter_taps, stations, allocation):
    length = filter_taps.shape[1]
    signals = voltages.shape[1]
    frames = voltages.shape[2] // length
    segments = lax.axis_size("tm")
    owners = lax.axis_size("wide")
    sub = lax.axis_index("tm")
    num_subs = stations.shape[0]
    ch_dev = length // owners
    wide_order = member_order(owners, WIDE_FIRST % owners)
    tm_order = member_order(segments, TM_FIRST % segments)

    table = jnp.asarray(transform_table(length, wide_order))
    x, tail, taps, table = stage(voltages, filter_taps, table)
    halo = shifted(tail, "tm", 1)
    body = filter_body(x, taps)
    spectra = transform(body, halo, x, taps, table)
    turned = exchange(spectra.reshape(owners, 2 * ch_dev, signals, frames), "wide", wide_order)

    by_owner = jnp.concatenate([stations[which : which + 1] for which in tm_order], axis=0)
    rows = (2 * by_owner[:, :, None] + jnp.arange(2, dtype=jnp.int32)[None, None, :]).reshape(-1, 1)
    held = np.asarray(wide_order)[:, None] * signals + np.arange(signals)[None, :]
    held = jnp.asarray(held.reshape(1, -1), jnp.int32)
    mine = lax.dynamic_slice(allocation, (sub, lax.axis_index("wide") * ch_dev), (1, ch_dev)).reshape(ch_dev)
    weights = mine.astype(jnp.float32) * (1.0 / (frames * segments))

    chosen = choose(rows, held, turned, num_subs)
    return correlate(weights, exchange(chosen, "tm", tm_order))


def solution(mesh):
    return jax.shard_map(
        shards,
        mesh=mesh,
        in_specs=(P(None, "wide", "tm"), P(), P(), P()),
        out_specs=P("tm", "wide", None, None, None),
        check_vma=False,
    )
```

```python
import math

import jax
import jax.numpy as jnp
import numpy as np
from jax import lax
from jax.experimental import pallas as pl
from jax.experimental.pallas import tpu as pltpu
from jax.sharding import PartitionSpec as P

LANES = 128
BLOCK = 16
WIDE_FIRST = 76
TM_FIRST = 1
IN_VMEM = pl.BlockSpec(memory_space=pltpu.VMEM)
IN_HBM = pl.BlockSpec(memory_space=pltpu.HBM)
IN_SMEM = pl.BlockSpec(memory_space=pltpu.SMEM)
PARAMS = pltpu.CompilerParams(vmem_limit_bytes=24 * 1024 * 1024)
CONTRACT_LAST = (((1,), (1,)), ((), ()))


def shifted(value, axis, steps):
    count = lax.axis_size(axis)
    initial, last = (max(0, -steps), min(count, count - steps))
    return lax.ppermute(value, axis, [(source, source + steps) for source in range(initial, last)])


def member_order(count, first):
    return [(first + step) % count for step in range(count)]


def exchange(value, axis, order):
    return lax.all_to_all(value, axis, split_axis=0, concat_axis=0, tiled=True, axis_index_groups=[order])


def transform_table(length, order):
    grid = np.arange(length)[:, None] * np.arange(length)[None, :] % length
    angle = grid * (2.0 * math.pi / length)
    scale = 1.0 / math.sqrt(length)
    cosine, sine = np.cos(angle) * scale, np.sin(angle) * scale
    real = np.concatenate([cosine, sine], axis=1)
    imaginary = np.concatenate([-sine, cosine], axis=1)
    table = np.stack([real, imaginary], axis=1).reshape(len(order), -1, 2 * length)[np.asarray(order)]
    return table.reshape(2 * length, 2 * length).astype(jnp.bfloat16)


def stage_kernel(x_ref, *refs):
    count = len(refs) // 2
    sources, tail_out, targets, sems = refs[: count - 1], refs[count - 1], refs[count:-1], refs[-1]
    first = x_ref.shape[2] - tail_out.shape[2]
    copies = [pltpu.make_async_copy(x_ref.at[:, :, first:], tail_out, sems.at[0])]
    for place, (source, target) in enumerate(zip((x_ref,) + sources, targets)):
        copies.append(pltpu.make_async_copy(source, target, sems.at[place + 1]))
    for copy in copies:
        copy.start()
    for copy in copies:
        copy.wait()


def stage(tail_length, *operands):
    tail = operands[0].shape[:2] + (tail_length,)
    return pl.pallas_call(
        stage_kernel,
        in_specs=[IN_HBM] * len(operands),
        out_specs=[IN_VMEM] * (len(operands) + 1),
        out_shape=[pltpu.VMEM(tail, operands[0].dtype)]
        + [pltpu.VMEM(value.shape, value.dtype) for value in operands],
        scratch_shapes=[pltpu.SemaphoreType.DMA((len(operands) + 1,))],
        compiler_params=PARAMS,
        name="stage",
    )(*[pltpu.with_memory_space_constraint(value, pltpu.HBM) for value in operands])


def load_frame(ref, part, frame, col, cols):
    start = (frame * cols + col) * LANES
    if not isinstance(start, int):
        start = pl.multiple_of(start, LANES)
    return ref[part, :, pl.ds(start, LANES)].astype(jnp.float32)


def tap_weights(taps_ref, col, signals):
    row = [taps_ref[tap : tap + 1, col * LANES : (col + 1) * LANES] for tap in range(taps_ref.shape[0])]
    return [jnp.broadcast_to(value, (signals, LANES)) for value in row]


def filter_frame(weights, window):
    total = weights[0] * window[0]
    for weight, value in zip(weights[1:], window[1:]):
        total = total + weight * value
    return total


def place_rows(stations_ref, places_ref, order, first, total):
    members = stations_ref.shape[1]
    for block, sub in enumerate(order):
        line = stations_ref[sub : sub + 1, :].astype(jnp.float32)
        station = jnp.broadcast_to(line, (members, members)).T.astype(jnp.int32)
        for pol in range(2):
            place = 2 * station + (pol - first)
            place = jnp.where(place < 0, place + total, place)
            places_ref[pl.ds(block * 2 * members + pol, members, stride=2), :] = place


def filter_kernel(x_ref, taps_ref, stations_ref, out_ref, places_ref, *, order, first, total):
    place_rows(stations_ref, places_ref, order, first, total)
    taps, length = taps_ref.shape
    signals = x_ref.shape[1]
    cols = length // LANES
    frames = x_ref.shape[2] // length
    for part in range(2):
        for col in range(cols):
            weights = tap_weights(taps_ref, col, signals)

            def step(block, window, part=part, col=col, weights=weights):
                first = block * BLOCK
                window = list(window) + [
                    load_frame(x_ref, part, first + frame, col, cols) for frame in range(BLOCK)
                ]
                for frame in range(BLOCK):
                    total = filter_frame(weights, window[frame : frame + taps])
                    out_ref[part, col, pl.ds(first + frame, signals, stride=frames), :] = total
                return tuple(window[BLOCK:])

            opening = tuple(
                load_frame(x_ref, part, BLOCK - (taps - 1) + frame, col, cols) for frame in range(taps - 1)
            )
            lax.fori_loop(1, frames // BLOCK, step, opening, unroll=frames // BLOCK - 1)


def filter_body(x, filter_taps, stations, **places):
    _, signals, samples = x.shape
    length = filter_taps.shape[1]
    members = stations.shape[1]
    shape = (2, length // LANES, signals * (samples // length), LANES)
    return pl.pallas_call(
        lambda *refs: filter_kernel(*refs, **places),
        in_specs=[IN_VMEM] * 3,
        out_specs=[IN_VMEM] * 2,
        out_shape=[pltpu.VMEM(shape, jnp.float32), pltpu.VMEM((2 * stations.size, members), jnp.int32)],
        compiler_params=PARAMS,
        cost_estimate=pl.CostEstimate(flops=12_000_000, bytes_accessed=6_000_000, transcendentals=0),
        name="filter_body",
    )(x, filter_taps, stations)


def transform_kernel(body_ref, halo_ref, x_ref, taps_ref, table_ref, out_ref, opening, turned):
    taps, length = taps_ref.shape
    signals = x_ref.shape[1]
    cols = length // LANES
    frames = x_ref.shape[2] // length
    for part in range(2):
        for col in range(cols):
            weights = tap_weights(taps_ref, col, signals)
            window = [load_frame(halo_ref, part, frame, col, cols) for frame in range(taps - 1)]
            window += [load_frame(x_ref, part, frame, col, cols) for frame in range(BLOCK)]
            for frame in range(BLOCK):
                total = filter_frame(weights, window[frame : frame + taps])
                opening[part, col, pl.ds(frame, signals, stride=BLOCK), :] = total

    rows = table_ref.shape[0]
    for pair in range(0, signals, 2):
        columns = []
        for part in range(2):
            for col in range(cols):
                pieces = []
                for signal in (pair, pair + 1):
                    pieces.append(opening[part, col, signal * BLOCK : (signal + 1) * BLOCK, :])
                    pieces.append(body_ref[part, col, signal * frames + BLOCK : (signal + 1) * frames, :])
                columns.append(jnp.concatenate(pieces, axis=0))
        samples = jnp.concatenate(columns, axis=1).astype(jnp.bfloat16)
        spectrum = lax.dot_general(table_ref[...], samples, CONTRACT_LAST, preferred_element_type=jnp.float32)
        for which in range(2):
            turned[pl.ds(pair + which, rows, stride=signals), :] = spectrum[
                :, which * frames : (which + 1) * frames
            ]
    out_ref[...] = turned[...].astype(jnp.bfloat16).reshape(out_ref.shape)


def transform(body, halo, x, filter_taps, table):
    taps, length = filter_taps.shape
    signals = x.shape[1]
    frames = x.shape[2] // length
    rows = table.shape[0]
    return pl.pallas_call(
        transform_kernel,
        in_specs=[IN_VMEM] * 5,
        out_specs=IN_VMEM,
        out_shape=pltpu.VMEM((rows, signals, frames), jnp.bfloat16),
        scratch_shapes=[
            pltpu.VMEM((2, length // LANES, signals * BLOCK, LANES), jnp.float32),
            pltpu.VMEM((rows * signals, frames), jnp.float32),
        ],
        compiler_params=PARAMS,
        cost_estimate=pl.CostEstimate(flops=540_000_000, bytes_accessed=4_000_000, transcendentals=0),
        name="transform",
    )(body, halo, x, filter_taps, table)


def choose_kernel(places_ref, x_ref, out_ref):
    sources, parts, signals, frames = x_ref.shape
    subs, _, members, _ = out_ref.shape
    width = places_ref.shape[1]
    columns = jnp.concatenate(
        [x_ref[:, part].reshape(sources * signals, frames) for part in range(parts)], axis=1
    )
    lane = lax.broadcasted_iota(jnp.int32, (members, width), 1)
    for sub in range(subs):
        wanted = places_ref[sub * members : (sub + 1) * members, :]
        pick = jnp.concatenate(
            [
                jnp.where(wanted == lane + start, 1.0, 0.0).astype(jnp.bfloat16)
                for start in range(0, sources * signals, width)
            ],
            axis=1,
        )
        chosen = jnp.dot(pick, columns, preferred_element_type=jnp.float32).astype(jnp.bfloat16)
        for part in range(parts):
            out_ref[sub, part] = chosen[:, part * frames : (part + 1) * frames]


def choose(places, turned, subs):
    _, parts, _, frames = turned.shape
    return pl.pallas_call(
        choose_kernel,
        in_specs=[IN_VMEM] * 2,
        out_specs=IN_VMEM,
        out_shape=pltpu.VMEM((subs, parts, places.shape[0] // subs, frames), jnp.bfloat16),
        compiler_params=PARAMS,
        cost_estimate=pl.CostEstimate(flops=1_100_000_000, bytes_accessed=2_000_000, transcendentals=0),
        name="choose",
    )(places, turned)


def correlate_kernel(allocation_ref, x_ref, out_ref, grams, sems):
    segments, parts, _, frames = x_ref.shape
    channels = parts // 2
    first = lax.axis_index("wide") * channels
    row = allocation_ref[pl.ds(lax.axis_index("tm"), 1), :].astype(jnp.float32) * (1.0 / (frames * segments))
    lane = lax.broadcasted_iota(jnp.int32, row.shape, 1)
    copies = []
    for channel in range(channels):
        real = [x_ref[segment, 2 * channel] for segment in range(segments)]
        imag = [x_ref[segment, 2 * channel + 1] for segment in range(segments)]
        left = jnp.concatenate(real + imag, axis=1)
        turned = jnp.concatenate(imag + [-value for value in real], axis=1)
        weight = jnp.sum(jnp.where(lane == first + channel, row, 0.0), axis=1, keepdims=True)
        for part, rows in enumerate((left, turned)):
            grams[channel, part] = weight * lax.dot_general(
                rows, left, CONTRACT_LAST, preferred_element_type=jnp.float32
            )
            copy = pltpu.make_async_copy(
                grams.at[channel, part], out_ref.at[0, channel, part], sems.at[2 * channel + part]
            )
            copy.start()
            copies.append(copy)
    for copy in copies:
        copy.wait()


def correlate(allocation, gathered):
    _, parts, members, _ = gathered.shape
    shape = (parts // 2, 2, members, members)
    return pl.pallas_call(
        correlate_kernel,
        in_specs=[IN_VMEM, IN_VMEM],
        out_specs=IN_HBM,
        out_shape=jax.ShapeDtypeStruct((1,) + shape, jnp.float32),
        scratch_shapes=[pltpu.VMEM(shape, jnp.float32), pltpu.SemaphoreType.DMA((parts,))],
        compiler_params=PARAMS,
        cost_estimate=pl.CostEstimate(flops=540_000_000, bytes_accessed=2_000_000, transcendentals=0),
        name="correlate",
    )(allocation, gathered)


def shards(voltages, filter_taps, stations, allocation):
    num_taps, length = filter_taps.shape
    signals = voltages.shape[1]
    frames = voltages.shape[2] // length
    owners = lax.axis_size("wide")
    wide_order = member_order(owners, WIDE_FIRST % owners)
    tm_order = member_order(lax.axis_size("tm"), TM_FIRST % lax.axis_size("tm"))

    table = jnp.asarray(transform_table(length, wide_order))
    tail, x, taps, table, stations, allocation = stage(
        (num_taps - 1) * length, voltages, filter_taps, table, stations, allocation
    )
    halo = shifted(tail, "tm", 1)
    body, places = filter_body(
        x, taps, stations, order=tm_order, first=wide_order[0] * signals, total=owners * signals
    )
    spectra = transform(body, halo, x, taps, table)
    spectra = spectra.reshape(owners, 2 * length // owners, signals, frames)
    turned = exchange(spectra, "wide", wide_order)
    chosen = choose(places, turned, stations.shape[0])
    return correlate(allocation, exchange(chosen, "tm", tm_order))


def solution(mesh):
    return jax.shard_map(
        shards,
        mesh=mesh,
        in_specs=(P(None, "wide", "tm"), P(), P(), P()),
        out_specs=P("tm", "wide", None, None, None),
        check_vma=False,
    )
```

```python
import math

import jax
import jax.numpy as jnp
import numpy as np
from jax import lax
from jax.experimental import pallas as pl
from jax.experimental.pallas import tpu as pltpu
from jax.sharding import PartitionSpec as P

LANES = 128
BLOCK = 16
WIDE_FIRST = 84
TM_FIRST = 2
IN_VMEM = pl.BlockSpec(memory_space=pltpu.VMEM)
IN_HBM = pl.BlockSpec(memory_space=pltpu.HBM)
IN_SMEM = pl.BlockSpec(memory_space=pltpu.SMEM)
PARAMS = pltpu.CompilerParams(vmem_limit_bytes=24 * 1024 * 1024)
CONTRACT_LAST = (((1,), (1,)), ((), ()))


def shifted(value, axis, steps):
    count = lax.axis_size(axis)
    initial, last = (max(0, -steps), min(count, count - steps))
    return lax.ppermute(value, axis, [(source, source + steps) for source in range(initial, last)])


def rolled(count, first):
    return [(first + step) % count for step in range(count)]


def interleaved(count, first):
    return [(first + step // 2 + step % 2 * (count // 2)) % count for step in range(count)]


def interleaved_place(signal, signals, count, first):
    half = signals * count // 2
    ahead = signal - first * signals
    ahead = jnp.where(ahead < 0, ahead + 2 * half, ahead)
    far = ahead >= half
    near = jnp.where(far, ahead - half, ahead)
    return 2 * near - near % signals + jnp.where(far, signals, 0)


def exchange(value, axis, order):
    return lax.all_to_all(value, axis, split_axis=0, concat_axis=0, tiled=True, axis_index_groups=[order])


def transform_table(length, order):
    grid = np.arange(length)[:, None] * np.arange(length)[None, :] % length
    angle = grid * (2.0 * math.pi / length)
    scale = 1.0 / math.sqrt(length)
    cosine, sine = np.cos(angle) * scale, np.sin(angle) * scale
    real = np.concatenate([cosine, sine], axis=1)
    imaginary = np.concatenate([-sine, cosine], axis=1)
    table = np.stack([real, imaginary], axis=1).reshape(len(order), -1, 2 * length)[np.asarray(order)]
    return table.reshape(2 * length, 2 * length).astype(jnp.bfloat16)


def place_rows(stations_ref, places_ref, order, place):
    members = stations_ref.shape[1]
    for block, sub in enumerate(order):
        line = stations_ref[sub : sub + 1, :].astype(jnp.float32)
        station = jnp.broadcast_to(line, (members, members)).T.astype(jnp.int32)
        for pol in range(2):
            places_ref[pl.ds(block * 2 * members + pol, members, stride=2), :] = place(2 * station + pol)


def stage_kernel(x_ref, taps_ref, stations_ref, allocation_ref, tail_out, x_out, taps_out, allocation_out, places_out,
                 stations, sems, *, order, place):
    first = x_ref.shape[2] - tail_out.shape[2]
    pairs = [
        (stations_ref, stations),
        (x_ref.at[:, :, first:], tail_out),
        (x_ref, x_out),
        (taps_ref, taps_out),
        (allocation_ref, allocation_out),
    ]
    copies = [pltpu.make_async_copy(*pair, sems.at[which]) for which, pair in enumerate(pairs)]
    for copy in copies:
        copy.start()
    copies[0].wait()
    place_rows(stations, places_out, order, place)
    for copy in copies[1:]:
        copy.wait()


def stage(voltages, filter_taps, stations, allocation, **rows):
    taps, length = filter_taps.shape
    members = stations.shape[1]
    operands = [voltages, filter_taps, stations, allocation]
    return pl.pallas_call(
        lambda *refs: stage_kernel(*refs, **rows),
        in_specs=[IN_HBM] * 4,
        out_specs=[IN_VMEM] * 5,
        out_shape=[
            pltpu.VMEM(voltages.shape[:2] + ((taps - 1) * length,), voltages.dtype),
            pltpu.VMEM(voltages.shape, voltages.dtype),
            pltpu.VMEM(filter_taps.shape, filter_taps.dtype),
            pltpu.VMEM(allocation.shape, allocation.dtype),
            pltpu.VMEM((2 * stations.size, members), jnp.int32),
        ],
        scratch_shapes=[pltpu.VMEM(stations.shape, stations.dtype), pltpu.SemaphoreType.DMA((5,))],
        compiler_params=PARAMS,
        name="stage",
    )(*[pltpu.with_memory_space_constraint(value, pltpu.HBM) for value in operands])


def load_frame(ref, part, frame, col, cols):
    start = (frame * cols + col) * LANES
    if not isinstance(start, int):
        start = pl.multiple_of(start, LANES)
    return ref[part, :, pl.ds(start, LANES)].astype(jnp.float32)


def tap_weights(taps_ref, col, signals):
    row = [taps_ref[tap : tap + 1, col * LANES : (col + 1) * LANES] for tap in range(taps_ref.shape[0])]
    return [jnp.broadcast_to(value, (signals, LANES)) for value in row]


def filter_frame(weights, window):
    total = weights[0] * window[0]
    for weight, value in zip(weights[1:], window[1:]):
        total = total + weight * value
    return total


def filter_kernel(x_ref, taps_ref, table_ref, out_ref, table_out, sem):
    copy = pltpu.make_async_copy(table_ref, table_out, sem)
    copy.start()
    taps, length = taps_ref.shape
    signals = x_ref.shape[1]
    cols = length // LANES
    frames = x_ref.shape[2] // length
    for part in range(2):
        for col in range(cols):
            weights = tap_weights(taps_ref, col, signals)

            def step(block, window, part=part, col=col, weights=weights):
                first = block * BLOCK
                window = list(window) + [
                    load_frame(x_ref, part, first + frame, col, cols) for frame in range(BLOCK)
                ]
                for frame in range(BLOCK):
                    total = filter_frame(weights, window[frame : frame + taps])
                    out_ref[part, col, pl.ds(first + frame, signals, stride=frames), :] = total
                return tuple(window[BLOCK:])

            opening = tuple(
                load_frame(x_ref, part, BLOCK - (taps - 1) + frame, col, cols) for frame in range(taps - 1)
            )
            lax.fori_loop(1, frames // BLOCK, step, opening, unroll=frames // BLOCK - 1)
    copy.wait()


def filter_body(x, filter_taps, table):
    _, signals, samples = x.shape
    length = filter_taps.shape[1]
    shape = (2, length // LANES, signals * (samples // length), LANES)
    return pl.pallas_call(
        filter_kernel,
        in_specs=[IN_VMEM, IN_VMEM, IN_HBM],
        out_specs=[IN_VMEM] * 2,
        out_shape=[pltpu.VMEM(shape, jnp.float32), pltpu.VMEM(table.shape, table.dtype)],
        scratch_shapes=[pltpu.SemaphoreType.DMA(())],
        compiler_params=PARAMS,
        cost_estimate=pl.CostEstimate(flops=12_000_000, bytes_accessed=6_000_000, transcendentals=0),
        name="filter_body",
    )(x, filter_taps, pltpu.with_memory_space_constraint(table, pltpu.HBM))


def transform_kernel(body_ref, halo_ref, x_ref, taps_ref, table_ref, out_ref, opening, turned):
    taps, length = taps_ref.shape
    signals = x_ref.shape[1]
    cols = length // LANES
    frames = x_ref.shape[2] // length
    for part in range(2):
        for col in range(cols):
            weights = tap_weights(taps_ref, col, signals)
            window = [load_frame(halo_ref, part, frame, col, cols) for frame in range(taps - 1)]
            window += [load_frame(x_ref, part, frame, col, cols) for frame in range(BLOCK)]
            for frame in range(BLOCK):
                total = filter_frame(weights, window[frame : frame + taps])
                opening[part, col, pl.ds(frame, signals, stride=BLOCK), :] = total

    rows = table_ref.shape[0]
    for pair in range(0, signals, 2):
        columns = []
        for part in range(2):
            for col in range(cols):
                pieces = []
                for signal in (pair, pair + 1):
                    pieces.append(opening[part, col, signal * BLOCK : (signal + 1) * BLOCK, :])
                    pieces.append(body_ref[part, col, signal * frames + BLOCK : (signal + 1) * frames, :])
                columns.append(jnp.concatenate(pieces, axis=0))
        samples = jnp.concatenate(columns, axis=1).astype(jnp.bfloat16)
        spectrum = lax.dot_general(table_ref[...], samples, CONTRACT_LAST, preferred_element_type=jnp.float32)
        for which in range(2):
            turned[pl.ds(pair + which, rows, stride=signals), :] = spectrum[
                :, which * frames : (which + 1) * frames
            ]
    out_ref[...] = turned[...].astype(jnp.bfloat16).reshape(out_ref.shape)


def transform(body, halo, x, filter_taps, table):
    taps, length = filter_taps.shape
    signals = x.shape[1]
    frames = x.shape[2] // length
    rows = table.shape[0]
    return pl.pallas_call(
        transform_kernel,
        in_specs=[IN_VMEM] * 5,
        out_specs=IN_VMEM,
        out_shape=pltpu.VMEM((rows, signals, frames), jnp.bfloat16),
        scratch_shapes=[
            pltpu.VMEM((2, length // LANES, signals * BLOCK, LANES), jnp.float32),
            pltpu.VMEM((rows * signals, frames), jnp.float32),
        ],
        compiler_params=PARAMS,
        cost_estimate=pl.CostEstimate(flops=540_000_000, bytes_accessed=4_000_000, transcendentals=0),
        name="transform",
    )(body, halo, x, filter_taps, table)


def choose_kernel(places_ref, x_ref, out_ref):
    sources, parts, signals, frames = x_ref.shape
    subs, _, members, _ = out_ref.shape
    width = places_ref.shape[1]
    columns = jnp.concatenate(
        [x_ref[:, part].reshape(sources * signals, frames) for part in range(parts)], axis=1
    )
    lane = lax.broadcasted_iota(jnp.int32, (members, width), 1)
    for sub in range(subs):
        wanted = places_ref[sub * members : (sub + 1) * members, :]
        pick = jnp.concatenate(
            [
                jnp.where(wanted == lane + start, 1.0, 0.0).astype(jnp.bfloat16)
                for start in range(0, sources * signals, width)
            ],
            axis=1,
        )
        chosen = jnp.dot(pick, columns, preferred_element_type=jnp.float32).astype(jnp.bfloat16)
        for part in range(parts):
            out_ref[sub, part] = chosen[:, part * frames : (part + 1) * frames]


def choose(places, turned, subs):
    _, parts, _, frames = turned.shape
    return pl.pallas_call(
        choose_kernel,
        in_specs=[IN_VMEM] * 2,
        out_specs=IN_VMEM,
        out_shape=pltpu.VMEM((subs, parts, places.shape[0] // subs, frames), jnp.bfloat16),
        compiler_params=PARAMS,
        cost_estimate=pl.CostEstimate(flops=1_100_000_000, bytes_accessed=2_000_000, transcendentals=0),
        name="choose",
    )(places, turned)


def correlate_kernel(allocation_ref, x_ref, out_ref, grams, sems):
    segments, parts, _, frames = x_ref.shape
    channels = parts // 2
    first = lax.axis_index("wide") * channels
    row = allocation_ref[pl.ds(lax.axis_index("tm"), 1), :].astype(jnp.float32) * (1.0 / (frames * segments))
    lane = lax.broadcasted_iota(jnp.int32, row.shape, 1)
    copies = []
    for channel in range(channels):
        real = [x_ref[segment, 2 * channel] for segment in range(segments)]
        imag = [x_ref[segment, 2 * channel + 1] for segment in range(segments)]
        left = jnp.concatenate(real + imag, axis=1)
        turned = jnp.concatenate(imag + [-value for value in real], axis=1)
        weight = jnp.sum(jnp.where(lane == first + channel, row, 0.0), axis=1, keepdims=True)
        for part, rows in enumerate((left, turned)):
            grams[channel, part] = weight * lax.dot_general(
                rows, left, CONTRACT_LAST, preferred_element_type=jnp.float32
            )
            copy = pltpu.make_async_copy(
                grams.at[channel, part], out_ref.at[0, channel, part], sems.at[2 * channel + part]
            )
            copy.start()
            copies.append(copy)
    for copy in copies:
        copy.wait()


def correlate(allocation, gathered):
    _, parts, members, _ = gathered.shape
    shape = (parts // 2, 2, members, members)
    return pl.pallas_call(
        correlate_kernel,
        in_specs=[IN_VMEM, IN_VMEM],
        out_specs=IN_HBM,
        out_shape=jax.ShapeDtypeStruct((1,) + shape, jnp.float32),
        scratch_shapes=[pltpu.VMEM(shape, jnp.float32), pltpu.SemaphoreType.DMA((parts,))],
        compiler_params=PARAMS,
        cost_estimate=pl.CostEstimate(flops=540_000_000, bytes_accessed=2_000_000, transcendentals=0),
        name="correlate",
    )(allocation, gathered)


def shards(voltages, filter_taps, stations, allocation):
    length = filter_taps.shape[1]
    signals = voltages.shape[1]
    frames = voltages.shape[2] // length
    owners = lax.axis_size("wide")
    first = WIDE_FIRST % owners
    wide_order = interleaved(owners, first)
    tm_order = rolled(lax.axis_size("tm"), TM_FIRST % lax.axis_size("tm"))

    tail, x, taps, allocation, places = stage(
        voltages,
        filter_taps,
        stations,
        allocation,
        order=tm_order,
        place=lambda signal: interleaved_place(signal, signals, owners, first),
    )
    halo = shifted(tail, "tm", 1)
    body, table = filter_body(x, taps, jnp.asarray(transform_table(length, wide_order)))
    spectra = transform(body, halo, x, taps, table)
    spectra = spectra.reshape(owners, 2 * length // owners, signals, frames)
    turned = exchange(spectra, "wide", wide_order)
    chosen = choose(places, turned, stations.shape[0])
    return correlate(allocation, exchange(chosen, "tm", tm_order))


def solution(mesh):
    return jax.shard_map(
        shards,
        mesh=mesh,
        in_specs=(P(None, "wide", "tm"), P(), P(), P()),
        out_specs=P("tm", "wide", None, None, None),
        check_vma=False,
    )
```

```python
import math

import jax
import jax.numpy as jnp
import numpy as np
from jax import lax
from jax.experimental import pallas as pl
from jax.experimental.pallas import tpu as pltpu
from jax.sharding import PartitionSpec as P

LANES = 128
BLOCK = 16
WIDE_FIRST = 84
ORDER = ((2,), (1, 3), (0,))
IN_VMEM = pl.BlockSpec(memory_space=pltpu.VMEM)
IN_HBM = pl.BlockSpec(memory_space=pltpu.HBM)
IN_SMEM = pl.BlockSpec(memory_space=pltpu.SMEM)
PARAMS = pltpu.CompilerParams(vmem_limit_bytes=24 * 1024 * 1024)
CONTRACT_LAST = (((1,), (1,)), ((), ()))


def shifted(value, axis, steps):
    count = lax.axis_size(axis)
    initial, last = (max(0, -steps), min(count, count - steps))
    return lax.ppermute(value, axis, [(source, source + steps) for source in range(initial, last)])


def interleaved(count, first):
    return [(first + step // 2 + step % 2 * (count // 2)) % count for step in range(count)]


def interleaved_place(signal, signals, count, first):
    half = signals * count // 2
    ahead = signal - first * signals
    ahead = jnp.where(ahead < 0, ahead + 2 * half, ahead)
    far = ahead >= half
    near = jnp.where(far, ahead - half, ahead)
    return 2 * near - near % signals + jnp.where(far, signals, 0)


def paired(value, axis, steps):
    count = lax.axis_size(axis)
    return lax.ppermute(value, axis, [(source, source ^ steps) for source in range(count)])


def exchange(value, axis, order):
    return lax.all_to_all(value, axis, split_axis=0, concat_axis=0, tiled=True, axis_index_groups=[order])


def transform_table(length, order):
    grid = np.arange(length)[:, None] * np.arange(length)[None, :] % length
    angle = grid * (2.0 * math.pi / length)
    scale = 1.0 / math.sqrt(length)
    cosine, sine = np.cos(angle) * scale, np.sin(angle) * scale
    real = np.concatenate([cosine, sine], axis=1)
    imaginary = np.concatenate([-sine, cosine], axis=1)
    table = np.stack([real, imaginary], axis=1).reshape(len(order), -1, 2 * length)[np.asarray(order)]
    return table.reshape(2 * length, 2 * length).astype(jnp.bfloat16)


def place_rows(stations_ref, places_ref, place):
    subs, members = stations_ref.shape
    own = lax.axis_index("tm")
    for block in range(subs):
        line = stations_ref[pl.ds(own ^ block, 1), :].astype(jnp.float32)
        station = jnp.broadcast_to(line, (members, members)).T.astype(jnp.int32)
        for pol in range(2):
            places_ref[pl.ds(block * 2 * members + pol, members, stride=2), :] = place(2 * station + pol)


def stage_kernel(x_ref, taps_ref, stations_ref, allocation_ref, tail_out, x_out, taps_out, allocation_out, places_out,
                 stations, sems, *, place):
    first = x_ref.shape[2] - tail_out.shape[2]
    pairs = [
        (stations_ref, stations),
        (x_ref.at[:, :, first:], tail_out),
        (x_ref, x_out),
        (taps_ref, taps_out),
        (allocation_ref, allocation_out),
    ]
    copies = [pltpu.make_async_copy(*pair, sems.at[which]) for which, pair in enumerate(pairs)]
    for copy in copies:
        copy.start()
    copies[0].wait()
    place_rows(stations, places_out, place)
    for copy in copies[1:]:
        copy.wait()


def stage(voltages, filter_taps, stations, allocation, **rows):
    taps, length = filter_taps.shape
    members = stations.shape[1]
    operands = [voltages, filter_taps, stations, allocation]
    return pl.pallas_call(
        lambda *refs: stage_kernel(*refs, **rows),
        in_specs=[IN_HBM] * 4,
        out_specs=[IN_VMEM] * 5,
        out_shape=[
            pltpu.VMEM(voltages.shape[:2] + ((taps - 1) * length,), voltages.dtype),
            pltpu.VMEM(voltages.shape, voltages.dtype),
            pltpu.VMEM(filter_taps.shape, filter_taps.dtype),
            pltpu.VMEM(allocation.shape, allocation.dtype),
            pltpu.VMEM((2 * stations.size, members), jnp.int32),
        ],
        scratch_shapes=[pltpu.VMEM(stations.shape, stations.dtype), pltpu.SemaphoreType.DMA((5,))],
        compiler_params=PARAMS,
        name="stage",
    )(*[pltpu.with_memory_space_constraint(value, pltpu.HBM) for value in operands])


def load_frame(ref, part, frame, col, cols):
    start = (frame * cols + col) * LANES
    if not isinstance(start, int):
        start = pl.multiple_of(start, LANES)
    return ref[part, :, pl.ds(start, LANES)].astype(jnp.float32)


def tap_weights(taps_ref, col, signals):
    row = [taps_ref[tap : tap + 1, col * LANES : (col + 1) * LANES] for tap in range(taps_ref.shape[0])]
    return [jnp.broadcast_to(value, (signals, LANES)) for value in row]


def filter_frame(weights, window):
    total = weights[0] * window[0]
    for weight, value in zip(weights[1:], window[1:]):
        total = total + weight * value
    return total


def filter_kernel(x_ref, taps_ref, table_ref, out_ref, table_out, sem):
    copy = pltpu.make_async_copy(table_ref, table_out, sem)
    copy.start()
    taps, length = taps_ref.shape
    signals = x_ref.shape[1]
    cols = length // LANES
    frames = x_ref.shape[2] // length
    for part in range(2):
        for col in range(cols):
            weights = tap_weights(taps_ref, col, signals)

            def step(block, window, part=part, col=col, weights=weights):
                first = block * BLOCK
                window = list(window) + [
                    load_frame(x_ref, part, first + frame, col, cols) for frame in range(BLOCK)
                ]
                for frame in range(BLOCK):
                    total = filter_frame(weights, window[frame : frame + taps])
                    out_ref[part, col, pl.ds(first + frame, signals, stride=frames), :] = total
                return tuple(window[BLOCK:])

            opening = tuple(
                load_frame(x_ref, part, BLOCK - (taps - 1) + frame, col, cols) for frame in range(taps - 1)
            )
            lax.fori_loop(1, frames // BLOCK, step, opening, unroll=frames // BLOCK - 1)
    copy.wait()


def filter_body(x, filter_taps, table):
    _, signals, samples = x.shape
    length = filter_taps.shape[1]
    shape = (2, length // LANES, signals * (samples // length), LANES)
    return pl.pallas_call(
        filter_kernel,
        in_specs=[IN_VMEM, IN_VMEM, IN_HBM],
        out_specs=[IN_VMEM] * 2,
        out_shape=[pltpu.VMEM(shape, jnp.float32), pltpu.VMEM(table.shape, table.dtype)],
        scratch_shapes=[pltpu.SemaphoreType.DMA(())],
        compiler_params=PARAMS,
        cost_estimate=pl.CostEstimate(flops=12_000_000, bytes_accessed=6_000_000, transcendentals=0),
        name="filter_body",
    )(x, filter_taps, pltpu.with_memory_space_constraint(table, pltpu.HBM))


def transform_kernel(body_ref, halo_ref, x_ref, taps_ref, table_ref, out_ref, opening, turned):
    taps, length = taps_ref.shape
    signals = x_ref.shape[1]
    cols = length // LANES
    frames = x_ref.shape[2] // length
    for part in range(2):
        for col in range(cols):
            weights = tap_weights(taps_ref, col, signals)
            window = [load_frame(halo_ref, part, frame, col, cols) for frame in range(taps - 1)]
            window += [load_frame(x_ref, part, frame, col, cols) for frame in range(BLOCK)]
            for frame in range(BLOCK):
                total = filter_frame(weights, window[frame : frame + taps])
                opening[part, col, pl.ds(frame, signals, stride=BLOCK), :] = total

    rows = table_ref.shape[0]
    for pair in range(0, signals, 2):
        columns = []
        for part in range(2):
            for col in range(cols):
                pieces = []
                for signal in (pair, pair + 1):
                    pieces.append(opening[part, col, signal * BLOCK : (signal + 1) * BLOCK, :])
                    pieces.append(body_ref[part, col, signal * frames + BLOCK : (signal + 1) * frames, :])
                columns.append(jnp.concatenate(pieces, axis=0))
        samples = jnp.concatenate(columns, axis=1).astype(jnp.bfloat16)
        spectrum = lax.dot_general(table_ref[...], samples, CONTRACT_LAST, preferred_element_type=jnp.float32)
        for which in range(2):
            turned[pl.ds(pair + which, rows, stride=signals), :] = spectrum[
                :, which * frames : (which + 1) * frames
            ]
    out_ref[...] = turned[...].astype(jnp.bfloat16).reshape(out_ref.shape)


def transform(body, halo, x, filter_taps, table):
    taps, length = filter_taps.shape
    signals = x.shape[1]
    frames = x.shape[2] // length
    rows = table.shape[0]
    return pl.pallas_call(
        transform_kernel,
        in_specs=[IN_VMEM] * 5,
        out_specs=IN_VMEM,
        out_shape=pltpu.VMEM((rows, signals, frames), jnp.bfloat16),
        scratch_shapes=[
            pltpu.VMEM((2, length // LANES, signals * BLOCK, LANES), jnp.float32),
            pltpu.VMEM((rows * signals, frames), jnp.float32),
        ],
        compiler_params=PARAMS,
        cost_estimate=pl.CostEstimate(flops=540_000_000, bytes_accessed=4_000_000, transcendentals=0),
        name="transform",
    )(body, halo, x, filter_taps, table)


def choose_kernel(places_ref, x_ref, *out_refs, blocks):
    sources, parts, signals, frames = x_ref.shape
    out_refs = out_refs[-len(blocks) :]
    members = out_refs[0].shape[1]
    width = places_ref.shape[1]
    columns = jnp.concatenate(
        [x_ref[:, part].reshape(sources * signals, frames) for part in range(parts)], axis=1
    )
    lane = lax.broadcasted_iota(jnp.int32, (members, width), 1)
    for block, out_ref in zip(blocks, out_refs):
        wanted = places_ref[block * members : (block + 1) * members, :]
        pick = jnp.concatenate(
            [
                jnp.where(wanted == lane + start, 1.0, 0.0).astype(jnp.bfloat16)
                for start in range(0, sources * signals, width)
            ],
            axis=1,
        )
        chosen = jnp.dot(pick, columns, preferred_element_type=jnp.float32).astype(jnp.bfloat16)
        for part in range(parts):
            out_ref[part] = chosen[:, part * frames : (part + 1) * frames]


def choose(places, turned, members, blocks, after=()):
    _, parts, _, frames = turned.shape
    return pl.pallas_call(
        lambda *refs: choose_kernel(*refs, blocks=blocks),
        in_specs=[IN_VMEM] * (2 + len(after)),
        out_specs=[IN_VMEM] * len(blocks),
        out_shape=[pltpu.VMEM((parts, members, frames), jnp.bfloat16)] * len(blocks),
        compiler_params=PARAMS,
        cost_estimate=pl.CostEstimate(
            flops=270_000_000 * len(blocks), bytes_accessed=1_000_000 * len(blocks), transcendentals=0
        ),
        name="choose",
    )(places, turned, *after)


def stacked(x_refs, channel):
    real = [segment[2 * channel] for segment in x_refs]
    imag = [segment[2 * channel + 1] for segment in x_refs]
    left = jnp.concatenate(real + imag, axis=1)
    return left, (left, jnp.concatenate(imag + [-value for value in real], axis=1))


def begin_kernel(*refs):
    x_refs, out_ref = refs[:-1], refs[-1]
    for channel in range(out_ref.shape[0]):
        left, both = stacked(x_refs, channel)
        for part, rows in enumerate(both):
            out_ref[channel, part] = lax.dot_general(rows, left, CONTRACT_LAST, preferred_element_type=jnp.float32)


def begin(gathered):
    parts, members, _ = gathered[0].shape
    return pl.pallas_call(
        begin_kernel,
        in_specs=[IN_VMEM] * len(gathered),
        out_specs=IN_VMEM,
        out_shape=pltpu.VMEM((parts // 2, 2, members, members), jnp.float32),
        compiler_params=PARAMS,
        cost_estimate=pl.CostEstimate(flops=270_000_000, bytes_accessed=2_000_000, transcendentals=0),
        name="begin",
    )(*gathered)


def correlate_kernel(allocation_ref, begun_ref, *refs):
    x_refs, (out_ref, grams, sems) = refs[:-3], refs[-3:]
    parts, _, frames = x_refs[0].shape
    channels = parts // 2
    first = lax.axis_index("wide") * channels
    scale = 1.0 / (frames * lax.axis_size("tm"))
    row = allocation_ref[pl.ds(lax.axis_index("tm"), 1), :].astype(jnp.float32) * scale
    lane = lax.broadcasted_iota(jnp.int32, row.shape, 1)
    copies = []
    for channel in range(channels):
        left, both = stacked(x_refs, channel)
        weight = jnp.sum(jnp.where(lane == first + channel, row, 0.0), axis=1, keepdims=True)
        for part, rows in enumerate(both):
            grams[channel, part] = weight * (
                begun_ref[channel, part]
                + lax.dot_general(rows, left, CONTRACT_LAST, preferred_element_type=jnp.float32)
            )
            copy = pltpu.make_async_copy(
                grams.at[channel, part], out_ref.at[0, channel, part], sems.at[2 * channel + part]
            )
            copy.start()
            copies.append(copy)
    for copy in copies:
        copy.wait()


def correlate(allocation, begun, gathered):
    parts, members, _ = gathered[0].shape
    shape = (parts // 2, 2, members, members)
    return pl.pallas_call(
        correlate_kernel,
        in_specs=[IN_VMEM] * (2 + len(gathered)),
        out_specs=IN_HBM,
        out_shape=jax.ShapeDtypeStruct((1,) + shape, jnp.float32),
        scratch_shapes=[pltpu.VMEM(shape, jnp.float32), pltpu.SemaphoreType.DMA((parts,))],
        compiler_params=PARAMS,
        cost_estimate=pl.CostEstimate(flops=270_000_000, bytes_accessed=2_000_000, transcendentals=0),
        name="correlate",
    )(allocation, begun, *gathered)


def shards(voltages, filter_taps, stations, allocation):
    length = filter_taps.shape[1]
    signals = voltages.shape[1]
    frames = voltages.shape[2] // length
    owners = lax.axis_size("wide")
    first = WIDE_FIRST % owners
    wide_order = interleaved(owners, first)

    tail, x, taps, allocation, places = stage(
        voltages,
        filter_taps,
        stations,
        allocation,
        place=lambda signal: interleaved_place(signal, signals, owners, first),
    )
    halo = shifted(tail, "tm", 1)
    body, table = filter_body(x, taps, jnp.asarray(transform_table(length, wide_order)))
    spectra = transform(body, halo, x, taps, table)
    spectra = spectra.reshape(owners, 2 * length // owners, signals, frames)
    turned = exchange(spectra, "wide", wide_order)
    members = 2 * stations.shape[1]
    met, after = [], ()
    for blocks in ORDER:
        after = choose(places, turned, members, blocks, after[:1])
        met += [paired(value, "tm", block) if block else value for block, value in zip(blocks, after)]
    return correlate(allocation, begin([met[-1], met[0]]), met[1:-1])


def solution(mesh):
    return jax.shard_map(
        shards,
        mesh=mesh,
        in_specs=(P(None, "wide", "tm"), P(), P(), P()),
        out_specs=P("tm", "wide", None, None, None),
        check_vma=False,
    )
```

```python
import math

import jax
import jax.numpy as jnp
import numpy as np
from jax import lax
from jax.experimental import pallas as pl
from jax.experimental.pallas import tpu as pltpu
from jax.sharding import PartitionSpec as P

LANES = 128
BLOCK = 16
WIDE_FIRST = 85
ORDER = ((2,), (1, 3), (0,))
IN_VMEM = pl.BlockSpec(memory_space=pltpu.VMEM)
IN_HBM = pl.BlockSpec(memory_space=pltpu.HBM)
IN_SMEM = pl.BlockSpec(memory_space=pltpu.SMEM)
PARAMS = pltpu.CompilerParams(vmem_limit_bytes=24 * 1024 * 1024)
CONTRACT_LAST = (((1,), (1,)), ((), ()))


def shifted(value, axis, steps):
    count = lax.axis_size(axis)
    initial, last = (max(0, -steps), min(count, count - steps))
    return lax.ppermute(value, axis, [(source, source + steps) for source in range(initial, last)])


def interleaved(count, first):
    return [(first + step // 2 + step % 2 * (count // 2)) % count for step in range(count)]


def interleaved_place(signal, signals, count, first):
    half = signals * count // 2
    ahead = signal - first * signals
    ahead = jnp.where(ahead < 0, ahead + 2 * half, ahead)
    far = ahead >= half
    near = jnp.where(far, ahead - half, ahead)
    return 2 * near - near % signals + jnp.where(far, signals, 0)


def paired(value, axis, steps):
    count = lax.axis_size(axis)
    return lax.ppermute(value, axis, [(source, source ^ steps) for source in range(count)])


def exchange(value, axis, order):
    return lax.all_to_all(value, axis, split_axis=0, concat_axis=0, tiled=True, axis_index_groups=[order])


def transform_table(length, order):
    grid = np.arange(length)[:, None] * np.arange(length)[None, :] % length
    angle = grid * (2.0 * math.pi / length)
    scale = 1.0 / math.sqrt(length)
    cosine, sine = np.cos(angle) * scale, np.sin(angle) * scale
    real = np.concatenate([cosine, sine], axis=1)
    imaginary = np.concatenate([-sine, cosine], axis=1)
    table = np.stack([real, imaginary], axis=1).reshape(len(order), -1, 2 * length)[np.asarray(order)]
    return table.reshape(2 * length, 2 * length).astype(jnp.bfloat16)


def place_rows(stations_ref, places_ref, place):
    subs, members = stations_ref.shape
    own = lax.axis_index("tm")
    for block in range(subs):
        line = stations_ref[pl.ds(own ^ block, 1), :].astype(jnp.float32)
        station = jnp.broadcast_to(line, (members, members)).T.astype(jnp.int32)
        for pol in range(2):
            places_ref[pl.ds(block * 2 * members + pol, members, stride=2), :] = place(2 * station + pol)


def stage_kernel(x_ref, taps_ref, stations_ref, allocation_ref, tail_out, x_out, taps_out, allocation_out, places_out,
                 stations, sems, *, place):
    first = x_ref.shape[2] - tail_out.shape[2]
    pairs = [
        (stations_ref, stations),
        (x_ref.at[:, :, first:], tail_out),
        (x_ref, x_out),
        (taps_ref, taps_out),
        (allocation_ref, allocation_out),
    ]
    copies = [pltpu.make_async_copy(*pair, sems.at[which]) for which, pair in enumerate(pairs)]
    for copy in copies:
        copy.start()
    copies[0].wait()
    place_rows(stations, places_out, place)
    for copy in copies[1:]:
        copy.wait()


def stage(voltages, filter_taps, stations, allocation, **rows):
    taps, length = filter_taps.shape
    members = stations.shape[1]
    operands = [voltages, filter_taps, stations, allocation]
    return pl.pallas_call(
        lambda *refs: stage_kernel(*refs, **rows),
        in_specs=[IN_HBM] * 4,
        out_specs=[IN_VMEM] * 5,
        out_shape=[
            pltpu.VMEM(voltages.shape[:2] + ((taps - 1) * length,), voltages.dtype),
            pltpu.VMEM(voltages.shape, voltages.dtype),
            pltpu.VMEM(filter_taps.shape, filter_taps.dtype),
            pltpu.VMEM(allocation.shape, allocation.dtype),
            pltpu.VMEM((2 * stations.size, members), jnp.int32),
        ],
        scratch_shapes=[pltpu.VMEM(stations.shape, stations.dtype), pltpu.SemaphoreType.DMA((5,))],
        compiler_params=PARAMS,
        name="stage",
    )(*[pltpu.with_memory_space_constraint(value, pltpu.HBM) for value in operands])


def load_frame(ref, part, frame, col, cols):
    start = (frame * cols + col) * LANES
    if not isinstance(start, int):
        start = pl.multiple_of(start, LANES)
    return ref[part, :, pl.ds(start, LANES)].astype(jnp.float32)


def tap_weights(taps_ref, col, signals):
    row = [taps_ref[tap : tap + 1, col * LANES : (col + 1) * LANES] for tap in range(taps_ref.shape[0])]
    return [jnp.broadcast_to(value, (signals, LANES)) for value in row]


def filter_frame(weights, window):
    total = weights[0] * window[0]
    for weight, value in zip(weights[1:], window[1:]):
        total = total + weight * value
    return total


def filter_kernel(x_ref, taps_ref, table_ref, out_ref, table_out, sem):
    copy = pltpu.make_async_copy(table_ref, table_out, sem)
    copy.start()
    taps, length = taps_ref.shape
    signals = x_ref.shape[1]
    cols = length // LANES
    frames = x_ref.shape[2] // length
    for part in range(2):
        for col in range(cols):
            weights = tap_weights(taps_ref, col, signals)

            def step(block, window, part=part, col=col, weights=weights):
                first = block * BLOCK
                window = list(window) + [
                    load_frame(x_ref, part, first + frame, col, cols) for frame in range(BLOCK)
                ]
                for frame in range(BLOCK):
                    total = filter_frame(weights, window[frame : frame + taps])
                    out_ref[part, col, pl.ds(first + frame, signals, stride=frames), :] = total
                return tuple(window[BLOCK:])

            opening = tuple(
                load_frame(x_ref, part, BLOCK - (taps - 1) + frame, col, cols) for frame in range(taps - 1)
            )
            lax.fori_loop(1, frames // BLOCK, step, opening, unroll=frames // BLOCK - 1)
    copy.wait()


def filter_body(x, filter_taps, table):
    _, signals, samples = x.shape
    length = filter_taps.shape[1]
    shape = (2, length // LANES, signals * (samples // length), LANES)
    return pl.pallas_call(
        filter_kernel,
        in_specs=[IN_VMEM, IN_VMEM, IN_HBM],
        out_specs=[IN_VMEM] * 2,
        out_shape=[pltpu.VMEM(shape, jnp.float32), pltpu.VMEM(table.shape, table.dtype)],
        scratch_shapes=[pltpu.SemaphoreType.DMA(())],
        compiler_params=PARAMS,
        cost_estimate=pl.CostEstimate(flops=12_000_000, bytes_accessed=6_000_000, transcendentals=0),
        name="filter_body",
    )(x, filter_taps, pltpu.with_memory_space_constraint(table, pltpu.HBM))


def transform_kernel(body_ref, halo_ref, x_ref, taps_ref, table_ref, out_ref, opening, turned):
    taps, length = taps_ref.shape
    signals = x_ref.shape[1]
    cols = length // LANES
    frames = x_ref.shape[2] // length
    for part in range(2):
        for col in range(cols):
            weights = tap_weights(taps_ref, col, signals)
            window = [load_frame(halo_ref, part, frame, col, cols) for frame in range(taps - 1)]
            window += [load_frame(x_ref, part, frame, col, cols) for frame in range(BLOCK)]
            for frame in range(BLOCK):
                total = filter_frame(weights, window[frame : frame + taps])
                opening[part, col, pl.ds(frame, signals, stride=BLOCK), :] = total

    rows = table_ref.shape[0]
    for pair in range(0, signals, 2):
        columns = []
        for part in range(2):
            for col in range(cols):
                pieces = []
                for signal in (pair, pair + 1):
                    pieces.append(opening[part, col, signal * BLOCK : (signal + 1) * BLOCK, :])
                    pieces.append(body_ref[part, col, signal * frames + BLOCK : (signal + 1) * frames, :])
                columns.append(jnp.concatenate(pieces, axis=0))
        samples = jnp.concatenate(columns, axis=1).astype(jnp.bfloat16)
        spectrum = lax.dot_general(table_ref[...], samples, CONTRACT_LAST, preferred_element_type=jnp.float32)
        for which in range(2):
            turned[pl.ds(pair + which, rows, stride=signals), :] = spectrum[
                :, which * frames : (which + 1) * frames
            ]
    out_ref[...] = turned[...].astype(jnp.bfloat16).reshape(out_ref.shape)


def transform(body, halo, x, filter_taps, table):
    taps, length = filter_taps.shape
    signals = x.shape[1]
    frames = x.shape[2] // length
    rows = table.shape[0]
    return pl.pallas_call(
        transform_kernel,
        in_specs=[IN_VMEM] * 5,
        out_specs=IN_VMEM,
        out_shape=pltpu.VMEM((rows, signals, frames), jnp.bfloat16),
        scratch_shapes=[
            pltpu.VMEM((2, length // LANES, signals * BLOCK, LANES), jnp.float32),
            pltpu.VMEM((rows * signals, frames), jnp.float32),
        ],
        compiler_params=PARAMS,
        cost_estimate=pl.CostEstimate(flops=540_000_000, bytes_accessed=4_000_000, transcendentals=0),
        name="transform",
    )(body, halo, x, filter_taps, table)


def choose_kernel(places_ref, x_ref, *out_refs, blocks):
    sources, parts, signals, frames = x_ref.shape
    out_refs = out_refs[-len(blocks) :]
    members = out_refs[0].shape[1]
    width = places_ref.shape[1]
    columns = jnp.concatenate(
        [x_ref[:, part].reshape(sources * signals, frames) for part in range(parts)], axis=1
    )
    lane = lax.broadcasted_iota(jnp.int32, (members, width), 1)
    for block, out_ref in zip(blocks, out_refs):
        wanted = places_ref[block * members : (block + 1) * members, :]
        pick = jnp.concatenate(
            [
                jnp.where(wanted == lane + start, 1.0, 0.0).astype(jnp.bfloat16)
                for start in range(0, sources * signals, width)
            ],
            axis=1,
        )
        chosen = jnp.dot(pick, columns, preferred_element_type=jnp.float32).astype(jnp.bfloat16)
        for part in range(parts):
            out_ref[part] = chosen[:, part * frames : (part + 1) * frames]


def choose(places, turned, members, blocks, after=()):
    _, parts, _, frames = turned.shape
    return pl.pallas_call(
        lambda *refs: choose_kernel(*refs, blocks=blocks),
        in_specs=[IN_VMEM] * (2 + len(after)),
        out_specs=[IN_VMEM] * len(blocks),
        out_shape=[pltpu.VMEM((parts, members, frames), jnp.bfloat16)] * len(blocks),
        compiler_params=PARAMS,
        cost_estimate=pl.CostEstimate(
            flops=270_000_000 * len(blocks), bytes_accessed=1_000_000 * len(blocks), transcendentals=0
        ),
        name="choose",
    )(places, turned, *after)


def stacked(x_refs, channel):
    real = [segment[2 * channel] for segment in x_refs]
    imag = [segment[2 * channel + 1] for segment in x_refs]
    left = jnp.concatenate(real + imag, axis=1)
    return left, (left, jnp.concatenate(imag + [-value for value in real], axis=1))


def begin_kernel(*refs):
    x_refs, out_ref = refs[:-1], refs[-1]
    for channel in range(out_ref.shape[0]):
        left, both = stacked(x_refs, channel)
        for part, rows in enumerate(both):
            out_ref[channel, part] = lax.dot_general(rows, left, CONTRACT_LAST, preferred_element_type=jnp.float32)


def begin(gathered):
    parts, members, _ = gathered[0].shape
    return pl.pallas_call(
        begin_kernel,
        in_specs=[IN_VMEM] * len(gathered),
        out_specs=IN_VMEM,
        out_shape=pltpu.VMEM((parts // 2, 2, members, members), jnp.float32),
        compiler_params=PARAMS,
        cost_estimate=pl.CostEstimate(flops=270_000_000, bytes_accessed=2_000_000, transcendentals=0),
        name="begin",
    )(*gathered)


def correlate_kernel(allocation_ref, begun_ref, *refs):
    x_refs, (out_ref, grams, sems) = refs[:-3], refs[-3:]
    parts, _, frames = x_refs[0].shape
    channels = parts // 2
    first = lax.axis_index("wide") * channels
    scale = 1.0 / (frames * lax.axis_size("tm"))
    row = allocation_ref[pl.ds(lax.axis_index("tm"), 1), :].astype(jnp.float32) * scale
    lane = lax.broadcasted_iota(jnp.int32, row.shape, 1)
    copies = []
    for channel in range(channels):
        left, both = stacked(x_refs, channel)
        weight = jnp.sum(jnp.where(lane == first + channel, row, 0.0), axis=1, keepdims=True)
        for part, rows in enumerate(both):
            grams[channel, part] = weight * (
                begun_ref[channel, part]
                + lax.dot_general(rows, left, CONTRACT_LAST, preferred_element_type=jnp.float32)
            )
            copy = pltpu.make_async_copy(
                grams.at[channel, part], out_ref.at[0, channel, part], sems.at[2 * channel + part]
            )
            copy.start()
            copies.append(copy)
    for copy in copies:
        copy.wait()


def correlate(allocation, begun, gathered):
    parts, members, _ = gathered[0].shape
    shape = (parts // 2, 2, members, members)
    return pl.pallas_call(
        correlate_kernel,
        in_specs=[IN_VMEM] * (2 + len(gathered)),
        out_specs=IN_HBM,
        out_shape=jax.ShapeDtypeStruct((1,) + shape, jnp.float32),
        scratch_shapes=[pltpu.VMEM(shape, jnp.float32), pltpu.SemaphoreType.DMA((parts,))],
        compiler_params=PARAMS,
        cost_estimate=pl.CostEstimate(flops=270_000_000, bytes_accessed=2_000_000, transcendentals=0),
        name="correlate",
    )(allocation, begun, *gathered)


def shards(voltages, filter_taps, stations, allocation):
    length = filter_taps.shape[1]
    signals = voltages.shape[1]
    frames = voltages.shape[2] // length
    owners = lax.axis_size("wide")
    first = WIDE_FIRST % owners
    wide_order = interleaved(owners, first)

    tail, x, taps, allocation, places = stage(
        voltages,
        filter_taps,
        stations,
        allocation,
        place=lambda signal: interleaved_place(signal, signals, owners, first),
    )
    halo = shifted(tail, "tm", 1)
    body, table = filter_body(x, taps, jnp.asarray(transform_table(length, wide_order)))
    spectra = transform(body, halo, x, taps, table)
    spectra = spectra.reshape(owners, 2 * length // owners, signals, frames)
    turned = exchange(spectra, "wide", wide_order)
    members = 2 * stations.shape[1]
    met, after = [], ()
    for blocks in ORDER:
        after = choose(places, turned, members, blocks, after[:1])
        met += [paired(value, "tm", block) if block else value for block, value in zip(blocks, after)]
    return correlate(allocation, begin([met[-1], met[0]]), met[1:-1])


def solution(mesh):
    return jax.shard_map(
        shards,
        mesh=mesh,
        in_specs=(P(None, "wide", "tm"), P(), P(), P()),
        out_specs=P("tm", "wide", None, None, None),
        check_vma=False,
    )
```

```python
import math

import jax
import jax.numpy as jnp
import numpy as np
from jax import lax
from jax.experimental import pallas as pl
from jax.experimental.pallas import tpu as pltpu
from jax.sharding import PartitionSpec as P

LANES = 128
BLOCK = 16
WIDE_FIRST = 85
ORDER = ((2,), (1, 3), (0,))
IN_VMEM = pl.BlockSpec(memory_space=pltpu.VMEM)
IN_HBM = pl.BlockSpec(memory_space=pltpu.HBM)
IN_SMEM = pl.BlockSpec(memory_space=pltpu.SMEM)
PARAMS = pltpu.CompilerParams(vmem_limit_bytes=24 * 1024 * 1024)
CONTRACT_LAST = (((1,), (1,)), ((), ()))


def shifted(value, axis, steps):
    count = lax.axis_size(axis)
    initial, last = (max(0, -steps), min(count, count - steps))
    return lax.ppermute(value, axis, [(source, source + steps) for source in range(initial, last)])


def interleaved(count, first):
    return [(first + step // 2 + step % 2 * (count // 2)) % count for step in range(count)]


def interleaved_place(signal, signals, count, first):
    half = signals * count // 2
    ahead = signal - first * signals
    ahead = jnp.where(ahead < 0, ahead + 2 * half, ahead)
    far = ahead >= half
    near = jnp.where(far, ahead - half, ahead)
    return 2 * near - near % signals + jnp.where(far, signals, 0)


def paired(value, axis, steps):
    count = lax.axis_size(axis)
    return lax.ppermute(value, axis, [(source, source ^ steps) for source in range(count)])


def exchange(value, axis, order):
    return lax.all_to_all(value, axis, split_axis=0, concat_axis=0, tiled=True, axis_index_groups=[order])


def transform_table(length, order):
    grid = np.arange(length)[:, None] * np.arange(length)[None, :] % length
    angle = grid * (2.0 * math.pi / length)
    scale = 1.0 / math.sqrt(length)
    cosine, sine = np.cos(angle) * scale, np.sin(angle) * scale
    real = np.concatenate([cosine, sine], axis=1)
    imaginary = np.concatenate([-sine, cosine], axis=1)
    table = np.stack([real, imaginary], axis=1).reshape(len(order), -1, 2 * length)[np.asarray(order)]
    return table.reshape(2 * length, 2 * length).astype(jnp.bfloat16)


def place_rows(stations_ref, places_ref, place):
    subs, members = stations_ref.shape
    own = lax.axis_index("tm")
    for block in range(subs):
        line = stations_ref[pl.ds(own ^ block, 1), :].astype(jnp.float32)
        station = jnp.broadcast_to(line, (members, members)).T.astype(jnp.int32)
        for pol in range(2):
            places_ref[pl.ds(block * 2 * members + pol, members, stride=2), :] = place(2 * station + pol)


def stage_kernel(x_ref, taps_ref, stations_ref, allocation_ref, tail_out, x_out, taps_out, allocation_out, places_out,
                 stations, sems, *, place):
    first = x_ref.shape[2] - tail_out.shape[2]
    pairs = [
        (stations_ref, stations),
        (x_ref.at[:, :, first:], tail_out),
        (x_ref, x_out),
        (taps_ref, taps_out),
        (allocation_ref, allocation_out),
    ]
    copies = [pltpu.make_async_copy(*pair, sems.at[which]) for which, pair in enumerate(pairs)]
    for copy in copies:
        copy.start()
    copies[0].wait()
    place_rows(stations, places_out, place)
    for copy in copies[1:]:
        copy.wait()


def stage(voltages, filter_taps, stations, allocation, **rows):
    taps, length = filter_taps.shape
    members = stations.shape[1]
    operands = [voltages, filter_taps, stations, allocation]
    return pl.pallas_call(
        lambda *refs: stage_kernel(*refs, **rows),
        in_specs=[IN_HBM] * 4,
        out_specs=[IN_VMEM] * 5,
        out_shape=[
            pltpu.VMEM(voltages.shape[:2] + ((taps - 1) * length,), voltages.dtype),
            pltpu.VMEM(voltages.shape, voltages.dtype),
            pltpu.VMEM(filter_taps.shape, filter_taps.dtype),
            pltpu.VMEM(allocation.shape, allocation.dtype),
            pltpu.VMEM((2 * stations.size, members), jnp.int32),
        ],
        scratch_shapes=[pltpu.VMEM(stations.shape, stations.dtype), pltpu.SemaphoreType.DMA((5,))],
        compiler_params=PARAMS,
        name="stage",
    )(*[pltpu.with_memory_space_constraint(value, pltpu.HBM) for value in operands])


def load_frame(ref, part, frame, col, cols):
    start = (frame * cols + col) * LANES
    if not isinstance(start, int):
        start = pl.multiple_of(start, LANES)
    return ref[part, :, pl.ds(start, LANES)].astype(jnp.float32)


def tap_weights(taps_ref, col, signals):
    row = [taps_ref[tap : tap + 1, col * LANES : (col + 1) * LANES] for tap in range(taps_ref.shape[0])]
    return [jnp.broadcast_to(value, (signals, LANES)) for value in row]


def filter_frame(weights, window):
    total = weights[0] * window[0]
    for weight, value in zip(weights[1:], window[1:]):
        total = total + weight * value
    return total


def filter_kernel(x_ref, taps_ref, table_ref, out_ref, table_out, filtered, sem):
    copy = pltpu.make_async_copy(table_ref, table_out, sem)
    copy.start()
    taps, length = taps_ref.shape
    signals = x_ref.shape[1]
    cols = length // LANES
    frames = x_ref.shape[2] // length
    for part in range(2):
        for col in range(cols):
            weights = tap_weights(taps_ref, col, signals)

            def step(block, window, part=part, col=col, weights=weights):
                first = block * BLOCK
                window = list(window) + [
                    load_frame(x_ref, part, first + frame, col, cols) for frame in range(BLOCK)
                ]
                for frame in range(BLOCK):
                    total = filter_frame(weights, window[frame : frame + taps])
                    filtered[part, col, pl.ds(first + frame, signals, stride=frames), :] = total
                return tuple(window[BLOCK:])

            opening = tuple(
                load_frame(x_ref, part, BLOCK - (taps - 1) + frame, col, cols) for frame in range(taps - 1)
            )
            lax.fori_loop(1, frames // BLOCK, step, opening, unroll=frames // BLOCK - 1)
            place = (part * cols + col) * LANES
            out_ref[:, place : place + LANES] = filtered[part, col].astype(jnp.bfloat16)
    copy.wait()


def filter_body(x, filter_taps, table):
    _, signals, samples = x.shape
    length = filter_taps.shape[1]
    shape = (2, length // LANES, signals * (samples // length), LANES)
    return pl.pallas_call(
        filter_kernel,
        in_specs=[IN_VMEM, IN_VMEM, IN_HBM],
        out_specs=[IN_VMEM] * 2,
        out_shape=[pltpu.VMEM((shape[2], 2 * length), jnp.bfloat16), pltpu.VMEM(table.shape, table.dtype)],
        scratch_shapes=[pltpu.VMEM(shape, jnp.float32), pltpu.SemaphoreType.DMA(())],
        compiler_params=PARAMS,
        cost_estimate=pl.CostEstimate(flops=12_000_000, bytes_accessed=6_000_000, transcendentals=0),
        name="filter_body",
    )(x, filter_taps, pltpu.with_memory_space_constraint(table, pltpu.HBM))


def transform_kernel(body_ref, halo_ref, x_ref, taps_ref, table_ref, out_ref, opening, turned):
    taps, length = taps_ref.shape
    signals = x_ref.shape[1]
    cols = length // LANES
    frames = x_ref.shape[2] // length
    for part in range(2):
        for col in range(cols):
            weights = tap_weights(taps_ref, col, signals)
            window = [load_frame(halo_ref, part, frame, col, cols) for frame in range(taps - 1)]
            window += [load_frame(x_ref, part, frame, col, cols) for frame in range(BLOCK)]
            for frame in range(BLOCK):
                total = filter_frame(weights, window[frame : frame + taps])
                opening[part, col, pl.ds(frame, signals, stride=BLOCK), :] = total

    rows = table_ref.shape[0]
    for pair in range(0, signals, 2):
        pieces = []
        for signal in (pair, pair + 1):
            rows_of = slice(signal * BLOCK, (signal + 1) * BLOCK)
            start = [opening[part, col, rows_of, :] for part in range(2) for col in range(cols)]
            pieces.append(jnp.concatenate(start, axis=1).astype(jnp.bfloat16))
            pieces.append(body_ref[signal * frames + BLOCK : (signal + 1) * frames, :])
        samples = jnp.concatenate(pieces, axis=0)
        spectrum = lax.dot_general(table_ref[...], samples, CONTRACT_LAST, preferred_element_type=jnp.float32)
        for which in range(2):
            turned[pl.ds(pair + which, rows, stride=signals), :] = spectrum[
                :, which * frames : (which + 1) * frames
            ]
    out_ref[...] = turned[...].astype(jnp.bfloat16).reshape(out_ref.shape)


def transform(body, halo, x, filter_taps, table):
    taps, length = filter_taps.shape
    signals = x.shape[1]
    frames = x.shape[2] // length
    rows = table.shape[0]
    return pl.pallas_call(
        transform_kernel,
        in_specs=[IN_VMEM] * 5,
        out_specs=IN_VMEM,
        out_shape=pltpu.VMEM((rows, signals, frames), jnp.bfloat16),
        scratch_shapes=[
            pltpu.VMEM((2, length // LANES, signals * BLOCK, LANES), jnp.float32),
            pltpu.VMEM((rows * signals, frames), jnp.float32),
        ],
        compiler_params=PARAMS,
        cost_estimate=pl.CostEstimate(flops=540_000_000, bytes_accessed=4_000_000, transcendentals=0),
        name="transform",
    )(body, halo, x, filter_taps, table)


def choose_kernel(places_ref, x_ref, *out_refs, blocks):
    sources, parts, signals, frames = x_ref.shape
    out_refs = out_refs[-len(blocks) :]
    members = out_refs[0].shape[1]
    width = places_ref.shape[1]
    columns = jnp.concatenate(
        [x_ref[:, part].reshape(sources * signals, frames) for part in range(parts)], axis=1
    )
    lane = lax.broadcasted_iota(jnp.int32, (members, width), 1)
    for block, out_ref in zip(blocks, out_refs):
        wanted = places_ref[block * members : (block + 1) * members, :]
        pick = jnp.concatenate(
            [
                jnp.where(wanted == lane + start, 1.0, 0.0).astype(jnp.bfloat16)
                for start in range(0, sources * signals, width)
            ],
            axis=1,
        )
        chosen = jnp.dot(pick, columns, preferred_element_type=jnp.float32).astype(jnp.bfloat16)
        for part in range(parts):
            out_ref[part] = chosen[:, part * frames : (part + 1) * frames]


def choose(places, turned, members, blocks, after=()):
    _, parts, _, frames = turned.shape
    return pl.pallas_call(
        lambda *refs: choose_kernel(*refs, blocks=blocks),
        in_specs=[IN_VMEM] * (2 + len(after)),
        out_specs=[IN_VMEM] * len(blocks),
        out_shape=[pltpu.VMEM((parts, members, frames), jnp.bfloat16)] * len(blocks),
        compiler_params=PARAMS,
        cost_estimate=pl.CostEstimate(
            flops=270_000_000 * len(blocks), bytes_accessed=1_000_000 * len(blocks), transcendentals=0
        ),
        name="choose",
    )(places, turned, *after)


def stacked(x_refs, channel):
    real = [segment[2 * channel] for segment in x_refs]
    imag = [segment[2 * channel + 1] for segment in x_refs]
    left = jnp.concatenate(real + imag, axis=1)
    return left, (left, jnp.concatenate(imag + [-value for value in real], axis=1))


def begin_kernel(*refs):
    x_refs, out_ref = refs[:-1], refs[-1]
    for channel in range(out_ref.shape[0]):
        left, both = stacked(x_refs, channel)
        for part, rows in enumerate(both):
            out_ref[channel, part] = lax.dot_general(rows, left, CONTRACT_LAST, preferred_element_type=jnp.float32)


def begin(gathered):
    parts, members, _ = gathered[0].shape
    return pl.pallas_call(
        begin_kernel,
        in_specs=[IN_VMEM] * len(gathered),
        out_specs=IN_VMEM,
        out_shape=pltpu.VMEM((parts // 2, 2, members, members), jnp.float32),
        compiler_params=PARAMS,
        cost_estimate=pl.CostEstimate(flops=270_000_000, bytes_accessed=2_000_000, transcendentals=0),
        name="begin",
    )(*gathered)


def correlate_kernel(allocation_ref, begun_ref, *refs):
    x_refs, (out_ref, grams, sems) = refs[:-3], refs[-3:]
    parts, _, frames = x_refs[0].shape
    channels = parts // 2
    first = lax.axis_index("wide") * channels
    scale = 1.0 / (frames * lax.axis_size("tm"))
    row = allocation_ref[pl.ds(lax.axis_index("tm"), 1), :].astype(jnp.float32) * scale
    lane = lax.broadcasted_iota(jnp.int32, row.shape, 1)
    copies = []
    for channel in range(channels):
        left, both = stacked(x_refs, channel)
        weight = jnp.sum(jnp.where(lane == first + channel, row, 0.0), axis=1, keepdims=True)
        for part, rows in enumerate(both):
            grams[channel, part] = weight * (
                begun_ref[channel, part]
                + lax.dot_general(rows, left, CONTRACT_LAST, preferred_element_type=jnp.float32)
            )
            copy = pltpu.make_async_copy(
                grams.at[channel, part], out_ref.at[0, channel, part], sems.at[2 * channel + part]
            )
            copy.start()
            copies.append(copy)
    for copy in copies:
        copy.wait()


def correlate(allocation, begun, gathered):
    parts, members, _ = gathered[0].shape
    shape = (parts // 2, 2, members, members)
    return pl.pallas_call(
        correlate_kernel,
        in_specs=[IN_VMEM] * (2 + len(gathered)),
        out_specs=IN_HBM,
        out_shape=jax.ShapeDtypeStruct((1,) + shape, jnp.float32),
        scratch_shapes=[pltpu.VMEM(shape, jnp.float32), pltpu.SemaphoreType.DMA((parts,))],
        compiler_params=PARAMS,
        cost_estimate=pl.CostEstimate(flops=270_000_000, bytes_accessed=2_000_000, transcendentals=0),
        name="correlate",
    )(allocation, begun, *gathered)


def shards(voltages, filter_taps, stations, allocation):
    length = filter_taps.shape[1]
    signals = voltages.shape[1]
    frames = voltages.shape[2] // length
    owners = lax.axis_size("wide")
    first = WIDE_FIRST % owners
    wide_order = interleaved(owners, first)

    tail, x, taps, allocation, places = stage(
        voltages,
        filter_taps,
        stations,
        allocation,
        place=lambda signal: interleaved_place(signal, signals, owners, first),
    )
    halo = shifted(tail, "tm", 1)
    body, table = filter_body(x, taps, jnp.asarray(transform_table(length, wide_order)))
    spectra = transform(body, halo, x, taps, table)
    spectra = spectra.reshape(owners, 2 * length // owners, signals, frames)
    turned = exchange(spectra, "wide", wide_order)
    members = 2 * stations.shape[1]
    met, after = [], ()
    for blocks in ORDER:
        after = choose(places, turned, members, blocks, after[:1])
        met += [paired(value, "tm", block) if block else value for block, value in zip(blocks, after)]
    return correlate(allocation, begin([met[-1], met[0]]), met[1:-1])


def solution(mesh):
    return jax.shard_map(
        shards,
        mesh=mesh,
        in_specs=(P(None, "wide", "tm"), P(), P(), P()),
        out_specs=P("tm", "wide", None, None, None),
        check_vma=False,
    )
```

```python
import math

import jax
import jax.numpy as jnp
import numpy as np
from jax import lax
from jax.experimental import pallas as pl
from jax.experimental.pallas import tpu as pltpu
from jax.sharding import PartitionSpec as P

LANES = 128
BLOCK = 16
WIDE_FIRST = 85
ORDER = ((2,), (1, 3), (0,))
IN_VMEM = pl.BlockSpec(memory_space=pltpu.VMEM)
IN_HBM = pl.BlockSpec(memory_space=pltpu.HBM)
IN_SMEM = pl.BlockSpec(memory_space=pltpu.SMEM)
PARAMS = pltpu.CompilerParams(vmem_limit_bytes=24 * 1024 * 1024)
CONTRACT_LAST = (((1,), (1,)), ((), ()))


def shifted(value, axis, steps):
    count = lax.axis_size(axis)
    initial, last = (max(0, -steps), min(count, count - steps))
    return lax.ppermute(value, axis, [(source, source + steps) for source in range(initial, last)])


def interleaved(count, first):
    return [(first + step // 2 + step % 2 * (count // 2)) % count for step in range(count)]


def interleaved_place(signal, signals, count, first):
    half = signals * count // 2
    ahead = signal - first * signals
    ahead = jnp.where(ahead < 0, ahead + 2 * half, ahead)
    far = ahead >= half
    near = jnp.where(far, ahead - half, ahead)
    return 2 * near - near % signals + jnp.where(far, signals, 0)


def paired(value, axis, steps):
    count = lax.axis_size(axis)
    return lax.ppermute(value, axis, [(source, source ^ steps) for source in range(count)])


def exchange(value, axis, order):
    return lax.all_to_all(value, axis, split_axis=0, concat_axis=0, tiled=True, axis_index_groups=[order])


def transform_table(length, order):
    grid = np.arange(length)[:, None] * np.arange(length)[None, :] % length
    angle = grid * (2.0 * math.pi / length)
    scale = 1.0 / math.sqrt(length)
    cosine, sine = np.cos(angle) * scale, np.sin(angle) * scale
    real = np.concatenate([cosine, sine], axis=1)
    imaginary = np.concatenate([-sine, cosine], axis=1)
    table = np.stack([real, imaginary], axis=1).reshape(len(order), -1, 2 * length)[np.asarray(order)]
    return table.reshape(2 * length, 2 * length).astype(jnp.bfloat16)


def place_rows(stations_ref, places_ref, place):
    subs, members = stations_ref.shape
    own = lax.axis_index("tm")
    for block in range(subs):
        line = stations_ref[pl.ds(own ^ block, 1), :].astype(jnp.float32)
        station = jnp.broadcast_to(line, (members, members)).T.astype(jnp.int32)
        for pol in range(2):
            places_ref[pl.ds(block * 2 * members + pol, members, stride=2), :] = place(2 * station + pol)


def stage_kernel(x_ref, taps_ref, stations_ref, allocation_ref, tail_out, x_out, taps_out, allocation_out, places_out,
                 stations, sems, *, place):
    first = x_ref.shape[2] - tail_out.shape[2]
    pairs = [
        (stations_ref, stations),
        (x_ref.at[:, :, first:], tail_out),
        (x_ref, x_out),
        (taps_ref, taps_out),
        (allocation_ref, allocation_out),
    ]
    copies = [pltpu.make_async_copy(*pair, sems.at[which]) for which, pair in enumerate(pairs)]
    for copy in copies:
        copy.start()
    copies[0].wait()
    place_rows(stations, places_out, place)
    for copy in copies[1:]:
        copy.wait()


def stage(voltages, filter_taps, stations, allocation, **rows):
    taps, length = filter_taps.shape
    members = stations.shape[1]
    operands = [voltages, filter_taps, stations, allocation]
    return pl.pallas_call(
        lambda *refs: stage_kernel(*refs, **rows),
        in_specs=[IN_HBM] * 4,
        out_specs=[IN_VMEM] * 5,
        out_shape=[
            pltpu.VMEM(voltages.shape[:2] + ((taps - 1) * length,), voltages.dtype),
            pltpu.VMEM(voltages.shape, voltages.dtype),
            pltpu.VMEM(filter_taps.shape, filter_taps.dtype),
            pltpu.VMEM(allocation.shape, allocation.dtype),
            pltpu.VMEM((2 * stations.size, members), jnp.int32),
        ],
        scratch_shapes=[pltpu.VMEM(stations.shape, stations.dtype), pltpu.SemaphoreType.DMA((5,))],
        compiler_params=PARAMS,
        name="stage",
    )(*[pltpu.with_memory_space_constraint(value, pltpu.HBM) for value in operands])


def load_frame(ref, part, frame, col, cols):
    start = (frame * cols + col) * LANES
    if not isinstance(start, int):
        start = pl.multiple_of(start, LANES)
    return ref[part, :, pl.ds(start, LANES)].astype(jnp.float32)


def tap_weights(taps_ref, col, signals):
    row = [taps_ref[tap : tap + 1, col * LANES : (col + 1) * LANES] for tap in range(taps_ref.shape[0])]
    return [jnp.broadcast_to(value, (signals, LANES)) for value in row]


def filter_frame(weights, window):
    total = weights[0] * window[0]
    for weight, value in zip(weights[1:], window[1:]):
        total = total + weight * value
    return total


def filter_kernel(x_ref, taps_ref, table_ref, out_ref, table_out, sem):
    copy = pltpu.make_async_copy(table_ref, table_out, sem)
    copy.start()
    taps, length = taps_ref.shape
    signals = x_ref.shape[1]
    cols = length // LANES
    frames = x_ref.shape[2] // length
    for part in range(2):
        for col in range(cols):
            weights = tap_weights(taps_ref, col, signals)

            def step(block, window, part=part, col=col, weights=weights):
                first = block * BLOCK
                window = list(window) + [
                    load_frame(x_ref, part, first + frame, col, cols) for frame in range(BLOCK)
                ]
                for frame in range(BLOCK):
                    total = filter_frame(weights, window[frame : frame + taps])
                    out_ref[part, col, pl.ds(first + frame, signals, stride=frames), :] = total
                return tuple(window[BLOCK:])

            opening = tuple(
                load_frame(x_ref, part, BLOCK - (taps - 1) + frame, col, cols) for frame in range(taps - 1)
            )
            lax.fori_loop(1, frames // BLOCK, step, opening, unroll=frames // BLOCK - 1)
    copy.wait()


def filter_body(x, filter_taps, table):
    _, signals, samples = x.shape
    length = filter_taps.shape[1]
    shape = (2, length // LANES, signals * (samples // length), LANES)
    return pl.pallas_call(
        filter_kernel,
        in_specs=[IN_VMEM, IN_VMEM, IN_HBM],
        out_specs=[IN_VMEM] * 2,
        out_shape=[pltpu.VMEM(shape, jnp.float32), pltpu.VMEM(table.shape, table.dtype)],
        scratch_shapes=[pltpu.SemaphoreType.DMA(())],
        compiler_params=PARAMS,
        cost_estimate=pl.CostEstimate(flops=12_000_000, bytes_accessed=6_000_000, transcendentals=0),
        name="filter_body",
    )(x, filter_taps, pltpu.with_memory_space_constraint(table, pltpu.HBM))


def transform_kernel(body_ref, halo_ref, x_ref, taps_ref, table_ref, out_ref, opening, turned):
    taps, length = taps_ref.shape
    signals = x_ref.shape[1]
    cols = length // LANES
    frames = x_ref.shape[2] // length
    for part in range(2):
        for col in range(cols):
            weights = tap_weights(taps_ref, col, signals)
            window = [load_frame(halo_ref, part, frame, col, cols) for frame in range(taps - 1)]
            window += [load_frame(x_ref, part, frame, col, cols) for frame in range(BLOCK)]
            for frame in range(BLOCK):
                total = filter_frame(weights, window[frame : frame + taps])
                opening[part, col, pl.ds(frame, signals, stride=BLOCK), :] = total

    rows = table_ref.shape[0]
    for pair in range(0, signals, 2):
        columns = []
        for part in range(2):
            for col in range(cols):
                pieces = []
                for signal in (pair, pair + 1):
                    pieces.append(opening[part, col, signal * BLOCK : (signal + 1) * BLOCK, :])
                    pieces.append(body_ref[part, col, signal * frames + BLOCK : (signal + 1) * frames, :])
                columns.append(jnp.concatenate(pieces, axis=0))
        samples = jnp.concatenate(columns, axis=1).astype(jnp.bfloat16)
        spectrum = lax.dot_general(table_ref[...], samples, CONTRACT_LAST, preferred_element_type=jnp.float32)
        for which in range(2):
            turned[pl.ds(pair + which, rows, stride=signals), :] = spectrum[
                :, which * frames : (which + 1) * frames
            ]
    out_ref[...] = turned[...].astype(jnp.bfloat16).reshape(out_ref.shape)


def transform(body, halo, x, filter_taps, table):
    taps, length = filter_taps.shape
    signals = x.shape[1]
    frames = x.shape[2] // length
    rows = table.shape[0]
    return pl.pallas_call(
        transform_kernel,
        in_specs=[IN_VMEM] * 5,
        out_specs=IN_VMEM,
        out_shape=pltpu.VMEM((rows, signals, frames), jnp.bfloat16),
        scratch_shapes=[
            pltpu.VMEM((2, length // LANES, signals * BLOCK, LANES), jnp.float32),
            pltpu.VMEM((rows * signals, frames), jnp.float32),
        ],
        compiler_params=PARAMS,
        cost_estimate=pl.CostEstimate(flops=540_000_000, bytes_accessed=4_000_000, transcendentals=0),
        name="transform",
    )(body, halo, x, filter_taps, table)


def choose_kernel(places_ref, x_ref, *out_refs, blocks):
    sources, parts, signals, frames = x_ref.shape
    out_refs = out_refs[-len(blocks) :]
    members = out_refs[0].shape[1]
    width = places_ref.shape[1]
    columns = jnp.concatenate(
        [x_ref[:, part].reshape(sources * signals, frames) for part in range(parts)], axis=1
    )
    lane = lax.broadcasted_iota(jnp.int32, (members, width), 1)
    for block, out_ref in zip(blocks, out_refs):
        wanted = places_ref[block * members : (block + 1) * members, :]
        pick = jnp.concatenate(
            [
                jnp.where(wanted == lane + start, 1.0, 0.0).astype(jnp.bfloat16)
                for start in range(0, sources * signals, width)
            ],
            axis=1,
        )
        chosen = jnp.dot(pick, columns, preferred_element_type=jnp.float32).astype(jnp.bfloat16)
        for part in range(parts):
            out_ref[part] = chosen[:, part * frames : (part + 1) * frames]


def choose(places, turned, members, blocks, after=()):
    _, parts, _, frames = turned.shape
    return pl.pallas_call(
        lambda *refs: choose_kernel(*refs, blocks=blocks),
        in_specs=[IN_VMEM] * (2 + len(after)),
        out_specs=[IN_VMEM] * len(blocks),
        out_shape=[pltpu.VMEM((parts, members, frames), jnp.bfloat16)] * len(blocks),
        compiler_params=PARAMS,
        cost_estimate=pl.CostEstimate(
            flops=270_000_000 * len(blocks), bytes_accessed=1_000_000 * len(blocks), transcendentals=0
        ),
        name="choose",
    )(places, turned, *after)


def stacked(x_refs, channel):
    real = [segment[2 * channel] for segment in x_refs]
    imag = [segment[2 * channel + 1] for segment in x_refs]
    left = jnp.concatenate(real + imag, axis=1)
    return left, (left, jnp.concatenate(imag + [-value for value in real], axis=1))


def begin_kernel(*refs):
    x_refs, out_ref = refs[:-1], refs[-1]
    for channel in range(out_ref.shape[0]):
        left, both = stacked(x_refs, channel)
        for part, rows in enumerate(both):
            out_ref[channel, part] = lax.dot_general(rows, left, CONTRACT_LAST, preferred_element_type=jnp.float32)


def begin(gathered):
    parts, members, _ = gathered[0].shape
    return pl.pallas_call(
        begin_kernel,
        in_specs=[IN_VMEM] * len(gathered),
        out_specs=IN_VMEM,
        out_shape=pltpu.VMEM((parts // 2, 2, members, members), jnp.float32),
        compiler_params=PARAMS,
        cost_estimate=pl.CostEstimate(flops=270_000_000, bytes_accessed=2_000_000, transcendentals=0),
        name="begin",
    )(*gathered)


def correlate_kernel(allocation_ref, begun_ref, *refs):
    x_refs, (out_ref, grams, sems) = refs[:-3], refs[-3:]
    parts, _, frames = x_refs[0].shape
    channels = parts // 2
    first = lax.axis_index("wide") * channels
    scale = 1.0 / (frames * lax.axis_size("tm"))
    row = allocation_ref[pl.ds(lax.axis_index("tm"), 1), :].astype(jnp.float32) * scale
    lane = lax.broadcasted_iota(jnp.int32, row.shape, 1)
    copies = []
    for channel in range(channels):
        left, both = stacked(x_refs, channel)
        weight = jnp.sum(jnp.where(lane == first + channel, row, 0.0), axis=1, keepdims=True)
        for part, rows in enumerate(both):
            grams[channel, part] = weight * (
                begun_ref[channel, part]
                + lax.dot_general(rows, left, CONTRACT_LAST, preferred_element_type=jnp.float32)
            )
            copy = pltpu.make_async_copy(
                grams.at[channel, part], out_ref.at[0, channel, part], sems.at[2 * channel + part]
            )
            copy.start()
            copies.append(copy)
    for copy in copies:
        copy.wait()


def correlate(allocation, begun, gathered):
    parts, members, _ = gathered[0].shape
    shape = (parts // 2, 2, members, members)
    return pl.pallas_call(
        correlate_kernel,
        in_specs=[IN_VMEM] * (2 + len(gathered)),
        out_specs=IN_HBM,
        out_shape=jax.ShapeDtypeStruct((1,) + shape, jnp.float32),
        scratch_shapes=[pltpu.VMEM(shape, jnp.float32), pltpu.SemaphoreType.DMA((parts,))],
        compiler_params=PARAMS,
        cost_estimate=pl.CostEstimate(flops=270_000_000, bytes_accessed=2_000_000, transcendentals=0),
        name="correlate",
    )(allocation, begun, *gathered)


def shards(voltages, filter_taps, stations, allocation):
    length = filter_taps.shape[1]
    signals = voltages.shape[1]
    frames = voltages.shape[2] // length
    owners = lax.axis_size("wide")
    first = WIDE_FIRST % owners
    wide_order = interleaved(owners, first)

    tail, x, taps, allocation, places = stage(
        voltages,
        filter_taps,
        stations,
        allocation,
        place=lambda signal: interleaved_place(signal, signals, owners, first),
    )
    halo = shifted(tail, "tm", 1)
    body, table = filter_body(x, taps, jnp.asarray(transform_table(length, wide_order)))
    spectra = transform(body, halo, x, taps, table)
    spectra = spectra.reshape(owners, 2 * length // owners, signals, frames)
    turned = exchange(spectra, "wide", wide_order)
    members = 2 * stations.shape[1]
    met, after = [], ()
    for blocks in ORDER:
        after = choose(places, turned, members, blocks, after[:1])
        met += [paired(value, "tm", block) if block else value for block, value in zip(blocks, after)]
    return correlate(allocation, begin([met[-1], met[0], met[2]]), met[1:2])


def solution(mesh):
    return jax.shard_map(
        shards,
        mesh=mesh,
        in_specs=(P(None, "wide", "tm"), P(), P(), P()),
        out_specs=P("tm", "wide", None, None, None),
        check_vma=False,
    )
```
